128 devices in a mesh: replica: 4 (over x), expert: 2 (over core), fsdp: 16 (over z, y).
Axes of the slice: x: 4, y: 4, z: 4, core: 2. Of those that a mesh axis runs over, the one named last changes fastest.
Arguments:
- tokens: bfloat16 [8, 4, 512, 768], P(('replica', 'expert'), None, 'fsdp'), may hold values from -6 to 6
- lengths: int32 [8, 4], P(('replica', 'expert')), may hold values from 1 to 512, 1280 in all within a row
- expert_ids: int32 [128, 128, 1], P(('replica', 'expert', 'fsdp')), may hold values from 0 to 3; in each aligned block of 128 rows (0 to 127, 128 to 255, ..., all dimensions but the last counted through in order) at most 64 rows name the same one
- gain_attn: bfloat16 [768], P('fsdp'), may hold values from 0.5 to 1.5
- w_query: bfloat16 [768, 768], P('fsdp'), may hold values from -0.02734375 to 0.02734375
- w_key: bfloat16 [768, 768], P('fsdp'), may hold values from -0.21875 to 0.21875
- w_value: bfloat16 [768, 768], P('fsdp'), may hold values from -0.21875 to 0.21875
- w_output: bfloat16 [768, 768], P('fsdp'), may hold values from -3.5 to 3.5
- rel_bias: bfloat16 [32, 12], P('fsdp'), may hold values from -4 to 4
- gain_ffn: bfloat16 [768], P('fsdp'), may hold values from 0.5 to 1.5
- router: bfloat16 [768, 4], P('fsdp'), may hold values from -0.15625 to 0.15625
- expert_in: bfloat16 [4, 3072, 768], P('expert', 'fsdp'), may hold values from -0.21875 to 0.21875
- expert_out: bfloat16 [4, 3072, 768], P('expert', 'fsdp'), may hold values from -0.4375 to 0.4375
- out_grad: bfloat16 [8, 4, 512, 768], P(('replica', 'expert'), None, 'fsdp'), may hold values from -6 to 6
Outputs:
- mixed: bfloat16 [8, 4, 512, 768], P(('replica', 'expert'), None, 'fsdp')
- grad_tokens: float32 [8, 4, 512, 768], P(('replica', 'expert'), None, 'fsdp')
- grad_gain_attn: float32 [768], P('fsdp')
- grad_query: float32 [768, 768], P('fsdp')
- grad_key: float32 [768, 768], P('fsdp')
- grad_value: float32 [768, 768], P('fsdp')
- grad_output: float32 [768, 768], P('fsdp')
- grad_rel_bias: float32 [32, 12], P('fsdp')
- grad_gain_ffn: float32 [768], P('fsdp')
- grad_router: float32 [768, 4], P('fsdp')
- grad_expert_in: float32 [4, 3072, 768], P('expert', 'fsdp')
- grad_expert_out: float32 [4, 3072, 768], P('expert', 'fsdp')
The draws below stay inside these ranges and needn't reach their ends.
Inputs may be any that keep to these rules, and one draw needn't show every extreme that they name: `expert_ids`: within the 128 rows of one device (one index of the first dimension) no expert is named more than 64 times, and in some device one expert is named exactly 64 times. Each group's 4 lengths sum to 1280, and one of them equals 512.
All inputs are finite; a program needn't handle non-finite values.
Results may differ from the reference program's by a relative error of at most 0.025.
Values may be sent and summed in bfloat16 or wider, within the bound.
A program may use at most 128 MiB of HBM per device.

```python
import math
import jax
import jax.numpy as jnp
import numpy as np
from jax import lax

D = 768
H = 12
HD = 64
FF = 3072
NB = 32
MAXDIST = 128
LMAX = 512
SEQ_GRP = 4
GROUPS = 8
SHARD_LEN = 32
ROWS = 128
EXPERTS = 4
CAP = 64
N_FSDP = 16
DEVICES = 128


def level_of(own_key, dims, shards, least, largest):
    gain, own = 1.0, jax.random.fold_in(own_key, 6)
    for dim, blocks in shards:
        steps = jnp.exp(jax.random.uniform(jax.random.fold_in(own, dim), (blocks,), jnp.float32, least / len(shards), largest / len(shards)))
        gain = gain * jnp.repeat(steps, dims[dim] // blocks).reshape([-1 if axis == dim else 1 for axis in range(len(dims))])
    return gain


def split_up(number_of, total, limit, skew):
    portions = [(1 << 20) // math.isqrt(standing ** skew) + 1 for standing in range(2, number_of + 1)]
    spare, counts = total - limit - (number_of - 1), [1] * (number_of - 1)
    while spare > 0:
        candidates = [i for i in range(number_of - 1) if counts[i] < limit]
        mass, left = sum([portions[i] for i in candidates]), spare
        for i in candidates:
            addition = min(limit - counts[i], max(1, left * portions[i] // mass), spare)
            counts[i] = counts[i] + addition
            spare = spare - addition
    return np.array([limit] + counts)


def ragged_sizes(rng, amount, total, most, lean):
    if amount == 2:
        one = jax.random.randint(rng, (), max(1, total - most), min(most, total - 1) + 1)
        return jnp.stack([one, total - one])
    sizes = jnp.asarray(split_up(amount, total, most, lean), jnp.int32)
    couples = (amount - 1) // 2
    giver, receiver = sizes[1:1 + 2 * couples:2], sizes[2:2 + 2 * couples:2]
    slack = jnp.minimum(giver - 1, most - receiver)
    passed = jax.random.randint(jax.random.fold_in(rng, 1), (couples,), 0, 1 << 20) % (slack + 1)
    sizes = sizes.at[1:1 + 2 * couples:2].set(giver - passed).at[2:2 + 2 * couples:2].set(receiver + passed)
    return sizes[jax.random.permutation(jax.random.fold_in(rng, 2), amount)]


def deal_out(rng, own, number, rows, number_of, top, limit, skew):
    order = jax.random.permutation(rng, number_of)
    packed, usual = shares(number_of, rows * top, limit, skew, True), shares(number_of, rows * top, limit, skew, False)
    places = jnp.arange(number_of)

    def named(sizes, turn):
        used = int((sizes > 0).sum())
        fixed = max(1, used // 4)
        moved = fixed + (places - fixed + turn * (used - fixed)) % max(1, number_of - fixed)
        return jnp.zeros((number_of,), jnp.int32).at[order[jnp.where(places < fixed, places, moved)]].set(jnp.asarray(sizes, jnp.int32))

    sizes = jnp.where(number % 4 == 0, named(packed, number // 4), named(usual, number - number // 4 - 1))
    mixed = jax.random.permutation(jax.random.fold_in(own, 3), number_of)
    giver, taker = mixed[0:number_of // 2 * 2:2], mixed[1:number_of // 2 * 2:2]
    margin = jnp.minimum(sizes[giver] - 1, limit - sizes[taker]) // 2
    margin = jnp.where((giver == order[0]) | (taker == order[0]) | (sizes[taker] == 0), 0, jnp.maximum(margin, 0))
    moved = jax.random.randint(jax.random.fold_in(own, 4), (number_of // 2,), 0, 1 << 20) % (margin + 1)
    sizes = sizes.at[giver].add(-moved).at[taker].add(moved)
    labels = jnp.searchsorted(jnp.cumsum(sizes), jnp.arange(rows * top), side="right").astype(jnp.int32)
    grid = labels.reshape(top, rows).T
    grid = grid[jax.random.permutation(jax.random.fold_in(own, 1), rows)]
    turn = jax.random.randint(jax.random.fold_in(own, 2), (rows, 1), 0, top)
    return jnp.take_along_axis(grid, (jnp.arange(top)[None, :] + turn) % top, axis=1)


def shares(amount, total, most, skew, full):
    loads = [(1 << 20) // math.isqrt(grade ** skew) + 1 for grade in range(1, amount + 1)]
    largest = most if full else min(most, max(-(-total // amount), total * loads[0] // sum(loads)))
    least = 1 if total - largest >= amount - 1 else 0
    counts, rest = [largest] + [least] * (amount - 1), total - largest - least * (amount - 1)
    while rest > 0:
        free = [i for i in range(1, amount) if counts[i] < largest] or [i for i in range(1, amount) if counts[i] < most]
        whole, remaining = sum([loads[i] for i in free]), rest
        for i in free:
            more = min(most - counts[i], max(1, remaining * loads[i] // whole), rest)
            counts[i] = counts[i] + more
            rest = rest - more
    return np.array(counts)


def normal_values(stream_key, extent, width, most, cuts=(), kind=jnp.bfloat16):
    entries = jax.random.normal(stream_key, extent, jnp.float32) * width
    if len(cuts) > 0:
        entries = level_of(stream_key, extent, cuts, -0.22, 0.18) * entries
    return jnp.clip(entries, min=-most, max=most).astype(kind)


def setup_inputs(seed: int = 0) -> dict:
    splits = jax.random.split(jax.random.key(seed), 15)
    tokens = normal_values(splits[0], (GROUPS, SEQ_GRP, LMAX, D), 1.0, 6.0, ((0, 8), (2, 16)))
    lengths = jax.vmap(lambda own: ragged_sizes(own, SEQ_GRP, LMAX + (SEQ_GRP - 1) * (LMAX // 2), LMAX, 2))(jax.random.split(splits[1], GROUPS)).reshape((GROUPS, SEQ_GRP)).astype(jnp.int32)
    expert_ids_keys = jax.random.split(jax.random.fold_in(splits[2], 1), DEVICES * ROWS // ROWS)
    expert_ids_turns = jax.random.permutation(jax.random.fold_in(splits[2], 3), DEVICES * ROWS // ROWS)
    expert_ids = jax.vmap(lambda own, number: deal_out(jax.random.fold_in(splits[2], 2), own, number, ROWS, EXPERTS, 1, CAP, 2))(expert_ids_keys, expert_ids_turns).reshape((DEVICES, ROWS, 1))
    gain_attn = jnp.clip(1.0 + 0.1 * jax.random.normal(splits[3], (D,), jnp.float32), 0.5, 1.5).astype(jnp.bfloat16)
    w_query = normal_values(splits[4], (D, D), (D * HD) ** -0.5, 0.02734375, ((0, 16),))
    w_key = normal_values(splits[5], (D, D), D ** -0.5, 0.21875, ((0, 16),))
    w_value = normal_values(splits[6], (D, D), D ** -0.5, 0.21875, ((0, 16),))
    w_output = normal_values(splits[7], (D, D), (max(D // 256, 1)) ** -0.5, 3.5, ((0, 16),))
    rel_bias = normal_values(splits[8], (NB, H), 1.0, 4.0, ((0, 16),))
    gain_ffn = jnp.clip(1.0 + 0.1 * jax.random.normal(splits[9], (D,), jnp.float32), 0.5, 1.5).astype(jnp.bfloat16)
    router = normal_values(splits[10], (D, EXPERTS), (2 * D) ** -0.5, 0.15625, ((0, 16),))
    expert_in = normal_values(splits[11], (EXPERTS, FF, D), D ** -0.5, 0.21875, ((0, 2), (1, 16)))
    expert_out = normal_values(splits[12], (EXPERTS, FF, D), (max(FF // (EXPERTS * EXPERTS), 1)) ** -0.5, 0.4375, ((0, 2), (1, 16)))
    out_grad = normal_values(splits[13], (GROUPS, SEQ_GRP, LMAX, D), 1.0, 6.0, ((0, 8), (2, 16)))
    return {"tokens": tokens, "lengths": lengths, "expert_ids": expert_ids, "gain_attn": gain_attn, "w_query": w_query, "w_key": w_key, "w_value": w_value, "w_output": w_output, "rel_bias": rel_bias, "gain_ffn": gain_ffn, "router": router, "expert_in": expert_in, "expert_out": expert_out, "out_grad": out_grad}


@jax.custom_vjp
def low(v):
    return lax.optimization_barrier(v.astype(jnp.bfloat16)).astype(jnp.float32)

@jax.custom_vjp
def low_back(v):
    return v

def low_keep(v):
    return (low(v), None)

def low_pass(kept, grad):
    return (grad,)

def back_keep(v):
    return (v, None)

def back_low(kept, grad):
    return (low(grad),)
low.defvjp(low_keep, low_pass)
low_back.defvjp(back_keep, back_low)
precise = lax.Precision.HIGHEST

def matmul(left_mat, right_mat):
    return jnp.dot(left_mat, right_mat, precision=precise)

def rms_norm(values, gain_vec):
    return values * lax.rsqrt(lax.optimization_barrier(jnp.mean(values * values, axis=-1, keepdims=True)) + 1e-06) * gain_vec

def bucket_table(length, buckets, distance):
    per_side = buckets // 2
    exact_span = per_side // 2
    near_list = []
    for dist in range(length):
        if dist < exact_span:
            near_list.append(dist)
        else:
            far_value = exact_span + int(math.log(dist / exact_span) / math.log(distance / exact_span) * (per_side - exact_span))
            near_list.append(min(far_value, per_side - 1))
    return [(per_side if offset > 0 else 0) + near_list[abs(offset)] for offset in range(-(length - 1), length)]

def bucket_onehot(query_pos, full_len, buckets):
    table = jnp.asarray(bucket_table(full_len, buckets, MAXDIST), dtype=jnp.int32)
    index = jnp.arange(full_len, dtype=jnp.int32)[None, :] - query_pos[:, None] + (full_len - 1)
    picked = jnp.take(table, index.astype(jnp.int32))
    onehot = (picked[..., None] == jnp.arange(buckets, dtype=jnp.int32)).astype(jnp.float32)
    return onehot.reshape(-1, buckets)

def to_device_order(array):
    return array.reshape(SEQ_GRP, N_FSDP, SHARD_LEN, -1).transpose(1, 0, 2, 3).reshape(N_FSDP, ROWS, -1)

def from_device_order(array):
    return array.reshape(N_FSDP, SEQ_GRP, SHARD_LEN, -1).transpose(1, 0, 2, 3).reshape(SEQ_GRP * LMAX, -1)

def group_layer(params, inputs, length_row, ids_dev, onehot):
    gain_one, wq_mat, wk_mat, wv_mat, wo_mat, bias_table, gain_two, router_mat, w_in, w_out = params
    flat = inputs.reshape(SEQ_GRP * LMAX, D)
    normed_one = low(rms_norm(flat, gain_one))
    query = low_back(low(matmul(normed_one, wq_mat)))
    key_rows = low_back(low(matmul(normed_one, wk_mat)))
    value_rows = low_back(low(matmul(normed_one, wv_mat)))
    bias = matmul(onehot, bias_table).reshape(LMAX, LMAX, H).transpose(2, 0, 1)

    def attend(item):
        query_seq, key_seq, value_seq, length = item
        query_heads = query_seq.reshape(LMAX, H, HD)
        key_heads = key_seq.reshape(LMAX, H, HD)
        value_heads = value_seq.reshape(LMAX, H, HD)
        scores = jnp.einsum('qhd,khd->hqk', query_heads, key_heads, precision=precise) + bias
        scores = low_back(scores)
        live = jnp.arange(LMAX, dtype=jnp.int32) < length
        scores = jnp.where(live[None, None, :], scores, -1e+30)
        topmost = lax.optimization_barrier(jnp.max(scores, axis=-1, keepdims=True))
        powers = jnp.exp(scores - topmost)
        probs = powers / lax.optimization_barrier(jnp.sum(powers, axis=-1, keepdims=True))
        attended = jnp.einsum('hqk,khd->qhd', low(probs), value_heads, precision=precise)
        return attended.reshape(LMAX, H * HD)
    attended = lax.map(jax.checkpoint(attend), (query.reshape(SEQ_GRP, LMAX, H * HD), key_rows.reshape(SEQ_GRP, LMAX, H * HD), value_rows.reshape(SEQ_GRP, LMAX, H * HD), length_row))
    attended = low_back(low(attended.reshape(SEQ_GRP * LMAX, H * HD)))
    branch = low_back(matmul(attended, wo_mat))
    hidden_one = flat + branch
    normed_two = low(rms_norm(hidden_one, gain_two))
    logits = matmul(normed_two, router_mat)
    router_probs = jax.nn.softmax(logits, axis=-1)
    chosen = (ids_dev[..., None] == jnp.arange(EXPERTS, dtype=jnp.int32)).astype(jnp.int32)
    gate = lax.optimization_barrier(jnp.sum(to_device_order(router_probs) * chosen.astype(jnp.float32), axis=-1))
    slot = lax.optimization_barrier(jnp.sum((jnp.cumsum(chosen, axis=1) - chosen) * chosen, axis=-1))
    dest = (jnp.arange(N_FSDP, dtype=jnp.int32)[:, None] * (EXPERTS * CAP) + ids_dev * CAP + slot).reshape(-1).astype(jnp.int32)
    dispatched = low_back(to_device_order(normed_two)).reshape(N_FSDP * ROWS, D)
    buffer = jnp.zeros((N_FSDP * EXPERTS * CAP, D), jnp.float32).at[dest].set(dispatched)
    buffer = buffer.reshape(N_FSDP, EXPERTS, CAP, D).transpose(1, 0, 2, 3).reshape(EXPERTS, N_FSDP * CAP, D)
    pre = low_back(jnp.einsum('erd,efd->erf', buffer, w_in, precision=precise))
    hidden = low(jax.nn.gelu(pre, approximate=False))
    result = low_back(low(jnp.einsum('erf,efd->erd', hidden, w_out, precision=precise)))
    result = result.reshape(EXPERTS, N_FSDP, CAP, D).transpose(1, 0, 2, 3).reshape(N_FSDP * EXPERTS * CAP, D)
    result_rows = jnp.take(result, dest, axis=0).reshape(N_FSDP, ROWS, D)
    moe = gate[..., None] * result_rows
    mixed = hidden_one + from_device_order(moe)
    return mixed.reshape(SEQ_GRP, LMAX, D)

def reference(tokens, lengths, expert_ids, gain_attn, w_query, w_key, w_value, w_output, rel_bias, gain_ffn, router, expert_in, expert_out, out_grad):
    params = tuple((item.astype(jnp.float32) for item in (gain_attn, w_query, w_key, w_value, w_output, rel_bias, gain_ffn, router, expert_in, expert_out)))
    onehot = bucket_onehot(jnp.arange(LMAX, dtype=jnp.int32), LMAX, NB)
    ids_all = expert_ids.reshape(GROUPS, N_FSDP, ROWS)

    def step(totals, item):
        inputs, cotangent, length_row, ids_dev = item

        def forward(param_set, values):
            return group_layer(param_set, values, length_row, ids_dev, onehot)
        mixed, pull_back = jax.vjp(forward, params, inputs.astype(jnp.float32))
        grad_params, grad_inputs = pull_back(cotangent.astype(jnp.float32))
        totals = jax.tree.map(lambda first, second: first + second, totals, grad_params)
        return (totals, (mixed.astype(jnp.bfloat16), grad_inputs))
    zeros = tuple((jnp.zeros_like(item) for item in params))
    totals, (mixed, grad_tokens) = lax.scan(step, zeros, (tokens, out_grad, lengths, ids_all))
    return (mixed, grad_tokens, totals[0], totals[1], totals[2], totals[3], totals[4], totals[5], totals[6], totals[7], totals[8], totals[9])
```

```python
import functools
import math

import jax
import jax.numpy as jnp
import numpy as np
from jax import lax
from jax.experimental import pallas as pl
from jax.experimental.pallas import tpu as pltpu
from jax.sharding import PartitionSpec as P

MAXDIST = 128
MESH = pl.DeviceIdType.MESH
F32, BF16 = jnp.float32, jnp.bfloat16
precise = lax.Precision.HIGHEST
VMEM_BYTES = 60 * 1024 * 1024

D, HEADS, HD, FF, NB, LEN, SEQS, SHARD, ROWS = 768, 12, 64, 3072, 32, 512, 4, 32, 128
EXPERTS, FSDP, UNITS = 4, 16, 192
HG = 3
HW = HG * HD


def bucket_of(offset):
    per_side, exact = NB // 2, NB // 4
    dist = abs(offset)
    if dist < exact:
        near = dist
    else:
        near = exact + int(math.log(dist / exact) / math.log(MAXDIST / exact) * (per_side - exact))
        near = min(near, per_side - 1)
    return (per_side if offset > 0 else 0) + near


def bucket_rows():
    onehot = np.zeros((2 * LEN, NB), np.float32)
    for index in range(2 * LEN):
        offset = index if index < LEN else index - 2 * LEN
        if offset != -LEN:
            onehot[index, bucket_of(offset)] = 1.0
    return onehot


def fsdp_peer(step, me):
    row = lax.rem(me // 4 + step // 4, 4)
    col = lax.rem(lax.rem(me, 4) + lax.rem(step, 4), 4)
    return row * 4 + col


def dot(left, right):
    return jnp.dot(left, right, preferred_element_type=F32)


def dot_rows(left, right):
    return lax.dot_general(left, right, (((0,), (0,)), ((), ())), preferred_element_type=F32)


def dot_last(left, right):
    return lax.dot_general(left, right, (((1,), (1,)), ((), ())), preferred_element_type=F32)


def gelu_pair(pre):
    cdf = 0.5 * (1.0 + lax.erf(pre * (2.0**-0.5)))
    pdf = jnp.exp(-0.5 * pre * pre) * (1.0 / math.sqrt(2.0 * math.pi))
    return pre * cdf, cdf + pre * pdf


def attention_forward(x_ref, gain, w_ref, bias_ref, bias_row, length, att_ref, probs_ref, qkv_ref, norm_ref):
    x = x_ref[...].reshape(LEN, D).astype(F32)
    scale = lax.rsqrt(jnp.mean(x * x, axis=-1, keepdims=True) + 1e-6)
    normed = (x * scale * gain).astype(BF16)
    norm_ref[...] = normed
    qkv_ref[...] = dot(normed, w_ref[...].reshape(D, 3 * HW)).astype(BF16)
    live = lax.broadcasted_iota(jnp.int32, (LEN, LEN), 1) < length
    for h in range(HG):
        query = qkv_ref[:, h * HD : (h + 1) * HD]
        key = qkv_ref[:, HW + h * HD : HW + (h + 1) * HD]
        value = qkv_ref[:, 2 * HW + h * HD : 2 * HW + (h + 1) * HD]
        line = jnp.broadcast_to(bias_ref[pl.ds(bias_row + h, 1), :], (LEN, 2 * LEN))
        bias = pltpu.roll(line, 0, 1, stride=1, stride_axis=0)[:, :LEN]
        scores = jnp.where(live, dot_last(query, key) + bias, -1e30)
        powers = jnp.exp(scores - jnp.max(scores, axis=-1, keepdims=True))
        probs = powers / jnp.sum(powers, axis=-1, keepdims=True)
        probs_ref[h] = probs
        att = dot(probs.astype(BF16), value).astype(BF16)
        att_ref[:, :, h * HD : (h + 1) * HD] = att.reshape(FSDP, SHARD, HD)


def unpack(small, place):
    wide = dot(small, place).reshape(FSDP, 16, D)
    owner = lax.broadcasted_iota(jnp.int32, (FSDP, 16, D), 2)
    first = lax.broadcasted_iota(jnp.int32, (FSDP, 16, D), 0) * 48
    return jnp.sum(jnp.where((owner >= first) & (owner < first + 48), wide, 0.0), axis=0)


def row_to_column(row):
    return jnp.broadcast_to(row.astype(F32), (ROWS, ROWS)).T[:, :1].astype(jnp.int32)


def front_kernel(
    length_ref, ids_ref, place_ref, bucket_ref, own_x_ref,
    gain_one_ref, gain_two_ref, router_in, bias_in, wq_ref, wk_ref, wv_ref,
    tokens, w_output, out_grad, ein, eout,
    x_out, w_out, wo_out, norm_out, qkv_out, att_out, probs_out, hidden_ref, router_ref, rows_ref,
    two_all, g_all, facts_all, win_all, wout_all,
    x_ref, w_ref, wo_ref, norm_ref, qkv_ref, att_ref, probs_ref, save,
    packed, small, small_ref, back_ref, bias_ref, two_ref, facts_ref,
    send, recv, local, pass_send, pass_recv, cross_send, cross_recv, relay_send, relay_recv,
):
    f, c, r = lax.axis_index("fsdp"), lax.axis_index("expert"), lax.axis_index("replica")
    z, y = f // 4, lax.rem(f, 4)
    other = 1 - c
    sibling = {"expert": other}
    in_col = lambda p: {"fsdp": p * 4 + y}
    in_row = lambda p: {"fsdp": z * 4 + p}
    barrier = pltpu.get_barrier_semaphore()

    def greet(where):
        pl.semaphore_signal(barrier, inc=1, device_id=where, device_id_type=MESH)

    def hello(step, carry):
        greet({"fsdp": fsdp_peer(step, f)})
        return carry

    lax.fori_loop(1, FSDP, hello, 0)
    greet(sibling)
    for step in range(1, 4):
        greet({"fsdp": lax.rem(z + step, 4) * 4 + y, "expert": other})
        greet({"replica": lax.rem(r + step, 4)})
    for h in range(4):
        for side, weight in enumerate((wq_ref, wk_ref, wv_ref)):
            packed[h, :, side * HW : (side + 1) * HW] = weight[:, h * HW : (h + 1) * HW]
    unit = lambda rows: (
        lax.broadcasted_iota(jnp.int32, (rows, 128), 0) == lax.broadcasted_iota(jnp.int32, (rows, 128), 1)
    ).astype(BF16)
    shift = lambda rows, by: (
        lax.broadcasted_iota(jnp.int32, (rows, 16), 0) + by == lax.broadcasted_iota(jnp.int32, (rows, 16), 1)
    ).astype(BF16)
    index = lax.broadcasted_iota(jnp.int32, (16, 128), 0)
    lines = dot_rows(shift(EXPERTS, 2), dot(router_in[...], unit(48)).astype(BF16))
    lines += dot_rows(shift(2, 6), dot(bias_in[...], unit(HEADS)).astype(BF16))
    lines += jnp.where(index == 0, dot(gain_one_ref[...], unit(48)), 0.0)
    lines += jnp.where(index == 1, dot(gain_two_ref[...], unit(48)), 0.0)
    small[...] = lines.astype(BF16)
    pl.semaphore_wait(barrier, FSDP - 1 + 7)

    def remote(k, src, dst, p, slot, where):
        return pltpu.make_async_remote_copy(
            src_ref=src, dst_ref=dst, send_sem=send.at[k, p], recv_sem=recv.at[k, slot],
            device_id=where, device_id_type=MESH,
        )

    def everyone(k, block, out):
        make = lambda p, slot: remote(k, block(p), out.at[slot], p, slot, {"fsdp": p})

        def push(step, carry):
            make(fsdp_peer(step, f), f).start()
            return carry

        def finish(step, carry):
            p = fsdp_peer(step, f)
            copy = make(p, p)
            copy.wait_recv()
            copy.wait_send()
            return carry

        own = pltpu.make_async_copy(block(f), out.at[f], local.at[k])
        lax.fori_loop(1, FSDP, push, 0)
        own.start()

        def wait():
            lax.fori_loop(1, FSDP, finish, 0)
            own.wait()

        return wait

    def ring(k, relay_k, src, out, me, where, cut, passed=lambda block, half: None):
        after, before, across = lax.rem(me + 1, 4), lax.rem(me + 3, 4), lax.rem(me + 2, 4)
        make = lambda p, slot: remote(k, src, out.at[slot], p, slot, where(p))

        def hand(block, half, p):
            there = cut(out.at[block], half)
            return pltpu.make_async_remote_copy(
                src_ref=there, dst_ref=there, send_sem=relay_send.at[relay_k, half],
                recv_sem=relay_recv.at[relay_k, half], device_id=where(p), device_id_type=MESH,
            )

        make(after, me).start()
        make(before, me).start()
        own = pltpu.make_async_copy(src, out.at[me], local.at[k])
        own.start()

        def relay():
            make(before, before).wait_recv()
            hand(before, 0, after).start()
            make(after, after).wait_recv()
            hand(after, 1, before).start()
            for block in (before, after):
                for half in range(2):
                    passed(block, half)

        def wait():
            for half, p in enumerate((after, before)):
                hand(across, half, p).wait_recv()
                passed(across, half)
            make(after, after).wait_send()
            make(before, before).wait_send()
            hand(before, 0, after).wait_send()
            hand(after, 1, before).wait_send()
            own.wait()

        return relay, wait

    def column(k, pass_k, src, out):
        def to_sibling(core, block, half, source=None):
            rows = pl.ds(half * (ROWS // 2), ROWS // 2)
            there = out.at[core * 4 + block, rows]
            return pltpu.make_async_remote_copy(
                src_ref=there if source is None else source.at[rows], dst_ref=there,
                send_sem=pass_send.at[pass_k, block, half], recv_sem=pass_recv.at[pass_k, block, half],
                device_id=sibling, device_id_type=MESH,
            )

        cut = lambda ref, half: ref.at[pl.ds(half * (ROWS // 2), ROWS // 2)]
        passed = lambda block, half: to_sibling(c, block, half).start()
        relay, wait_own = ring(k, pass_k, src, out.at[pl.ds(c * 4, 4)], z, in_col, cut, passed)
        for half in range(2):
            to_sibling(c, z, half, src).start()

        def wait():
            wait_own()
            for block in range(4):
                for half in range(2):
                    to_sibling(c, block, half).wait_send()
                    to_sibling(other, block, half).wait_recv()

        return relay, wait

    wait_x = everyone(0, lambda p: tokens.at[lax.rem(p, 4)], x_ref)
    wait_small = everyone(1, lambda p: small, small_ref)
    wait_w = everyone(2, lambda p: packed.at[p // 4], w_ref)
    quarter = pl.ds(pl.multiple_of(r * 48, 48), 48)
    ring_steps = (1, 3, 2)

    def fetch(p, slot):
        return remote(
            5, eout.at[:, quarter], wout_all.at[slot, :, quarter], p, slot, in_row(p)
        )

    def cross(block, q, part):
        rows = pl.ds(pl.multiple_of(part * 48, 48), 48)
        return pltpu.make_async_remote_copy(
            src_ref=wout_all.at[block, :, rows], dst_ref=wout_all.at[block, :, rows],
            send_sem=cross_send.at[block, q], recv_sem=cross_recv.at[block, part],
            device_id={"replica": q}, device_id_type=MESH,
        )

    for step in ring_steps:
        fetch(lax.rem(y + step, 4), y).start()
    own_wout = pltpu.make_async_copy(eout, wout_all.at[y], local.at[5])
    own_wout.start()

    def cross_all():
        for step in ring_steps:
            block = lax.rem(y + step, 4)
            fetch(block, block).wait_recv()
            for turn in ring_steps:
                cross(block, lax.rem(r + turn, 4), r).start()

    def wait_wout():
        own_wout.wait()
        for step in ring_steps:
            block = lax.rem(y + step, 4)
            fetch(block, block).wait_send()
            for turn in ring_steps:
                q = lax.rem(r + turn, 4)
                cross(block, q, r).wait_send()
                cross(block, q, q).wait_recv()


    wait_small()
    smalls = small_ref[...].reshape(FSDP * 16, 128)
    rows = unpack(smalls, place_ref[...].astype(BF16))
    rows_ref[...] = rows
    bias_ref[...] = dot_rows(smalls, bucket_ref[...].astype(BF16))[:16]
    wait_x()
    wait_w()
    wait_wo = everyone(3, lambda p: w_output, wo_ref)
    forward_g, wait_g = column(6, 0, out_grad, g_all)
    relay_win, wait_win = ring(
        4, 2, ein, win_all, y, in_row, lambda ref, half: ref.at[pl.ds(half, 1)]
    )
    attention_forward(
        x_ref, rows[0:1], w_ref, bias_ref, HG * z, length_ref[0, y], att_ref, probs_ref, qkv_ref, norm_ref
    )

    wait_att = everyone(7, lambda p: att_ref.at[p], back_ref)
    pairs = (
        (x_ref, x_out), (w_ref, w_out), (norm_ref, norm_out), (qkv_ref, qkv_out), (att_ref, att_out),
        (probs_ref, probs_out), (wo_ref, wo_out),
    )
    saves = [pltpu.make_async_copy(src, dst, save.at[k]) for k, (src, dst) in enumerate(pairs)]
    cross_all()
    forward_g()
    for copy in saves[:6]:
        copy.start()
    wait_wo()
    saves[6].start()
    wait_att()
    hidden = own_x_ref[...].astype(F32)
    for h in range(4):
        att = jnp.concatenate([back_ref[h * 4 + s] for s in range(SEQS)], axis=0)
        hidden += dot(att, wo_ref[4 * h : 4 * h + 4].reshape(HW, D))
    hidden_ref[...] = hidden
    scale = lax.rsqrt(jnp.mean(hidden * hidden, axis=-1, keepdims=True) + 1e-6)
    two = (hidden * scale * rows[1:2]).astype(BF16)
    two_ref[...] = two
    forward_two, wait_two = column(8, 1, two_ref, two_all)
    logits = lax.dot_general(
        two.astype(F32), rows, (((1,), (1,)), ((), ())), precision=precise, preferred_element_type=F32
    )
    lane = lax.broadcasted_iota(jnp.int32, (ROWS, 16), 1)
    inside = (lane >= 2) & (lane < 2 + EXPERTS)
    logits = jnp.where(inside, logits, -1e30)
    powers = jnp.where(inside, jnp.exp(logits - jnp.max(logits, axis=-1, keepdims=True)), 0.0)
    router_probs = powers / jnp.sum(powers, axis=-1, keepdims=True)
    router_ref[...] = router_probs
    ids = row_to_column(ids_ref[...])
    gate = jnp.sum(jnp.where(lane == ids + 2, router_probs, 0.0), axis=-1, keepdims=True)
    wide = lax.broadcasted_iota(jnp.int32, (ROWS, ROWS), 1)
    facts = jnp.where(wide == 0, gate, jnp.where(wide == 1, ids.astype(F32), 0.0))
    facts_ref[...] = facts.T[:8]
    me = c * 4 + z
    spots = [(other if i % 2 == 0 else c, lax.rem(z + (i + 1) // 2, 4)) for i in range(7)]
    fact = lambda core, p, slot: remote(
        9, facts_ref, facts_all.at[slot], core * 4 + p, slot, {"fsdp": p * 4 + y, "expert": core}
    )
    for core, p in spots:
        fact(core, p, me).start()
    own_facts = pltpu.make_async_copy(facts_ref, facts_all.at[me], local.at[9])
    own_facts.start()
    forward_two()
    relay_win()
    for copy in saves:
        copy.wait()
    wait_two()
    wait_g()
    wait_win()
    wait_wout()
    for core, p in spots:
        copy = fact(core, p, core * 4 + p)
        copy.wait_recv()
        copy.wait_send()
    own_facts.wait()


def front(lengths, *arrays):
    vmem, smem = pl.BlockSpec(memory_space=pltpu.VMEM), pl.BlockSpec(memory_space=pltpu.SMEM)
    anywhere = pl.BlockSpec(memory_space=pl.ANY)
    shape = jax.ShapeDtypeStruct
    return pl.pallas_call(
        front_kernel,
        out_shape=(
            shape((FSDP, SHARD, D), BF16),
            shape((FSDP, 48, 3 * HW), BF16),
            shape((FSDP, 48, D), BF16),
            shape((LEN, D), BF16),
            shape((LEN, 3 * HW), BF16),
            shape((FSDP, SHARD, HW), BF16),
            shape((HG, LEN, LEN), F32),
            shape((ROWS, D), F32),
            shape((ROWS, 16), F32),
            shape((16, D), F32),
            shape((8, ROWS, D), BF16),
            shape((8, ROWS, D), BF16),
            shape((8, 8, ROWS), F32),
            shape((4, 2, UNITS, D), BF16),
            shape((4, 2, UNITS, D), BF16),
        ),
        in_specs=[smem] + [vmem] * 11 + [anywhere] * 5,
        out_specs=(anywhere,) * 7 + (vmem,) * 3 + (anywhere,) * 5,
        scratch_shapes=[
            pltpu.VMEM((FSDP, SHARD, D), BF16),
            pltpu.VMEM((FSDP, 48, 3 * HW), BF16),
            pltpu.VMEM((FSDP, 48, D), BF16),
            pltpu.VMEM((LEN, D), BF16),
            pltpu.VMEM((LEN, 3 * HW), BF16),
            pltpu.VMEM((FSDP, SHARD, HW), BF16),
            pltpu.VMEM((HG, LEN, LEN), F32),
            pltpu.SemaphoreType.DMA((7,)),
            pltpu.VMEM((4, 48, 3 * HW), BF16),
            pltpu.VMEM((16, 128), BF16),
            pltpu.VMEM((FSDP, 16, 128), BF16),
            pltpu.VMEM((FSDP, SHARD, HW), BF16),
            pltpu.VMEM((16, 2 * LEN), F32),
            pltpu.VMEM((ROWS, D), BF16),
            pltpu.VMEM((8, ROWS), F32),
            pltpu.SemaphoreType.DMA((10, 16)),
            pltpu.SemaphoreType.DMA((10, 16)),
            pltpu.SemaphoreType.DMA((10,)),
            pltpu.SemaphoreType.DMA((2, 4, 2)),
            pltpu.SemaphoreType.DMA((2, 4, 2)),
            pltpu.SemaphoreType.DMA((4, 4)),
            pltpu.SemaphoreType.DMA((4, 4)),
            pltpu.SemaphoreType.DMA((3, 2)),
            pltpu.SemaphoreType.DMA((3, 2)),
        ],
        compiler_params=pltpu.CompilerParams(
            collective_id=0, has_side_effects=True, vmem_limit_bytes=VMEM_BYTES
        ),
        name="front",
    )(lengths, *arrays)


def rms_scale(values):
    return lax.rsqrt(jnp.mean(values * values, axis=-1, keepdims=True) + 1e-6)


def norm_back(values, scale, gain, upstream):
    weighted = upstream * gain
    inner = jnp.mean(values * weighted, axis=-1, keepdims=True)
    return scale * weighted - values * (scale * scale * scale * inner)


HALF = 4 * ROWS
STEP = 256
CHUNK = 64


def back_kernel(
    facts_ref, hidden_in, router_in, rows_in, own_x, own_g, ids_in, place_ref, bucket_ref,
    x_hbm, norm_hbm, wo_hbm, w_hbm, att_hbm, probs_hbm, qkv_hbm, two_hbm, g_hbm, win_hbm, wout_hbm,
    mixed_ref, gtokens_ref, dense_out, totals_out, gin3_ref, gout3_ref, gin1_ref, gout1_ref,
    w_ref, att_ref, probs_ref, qkv_ref, two_ref, g_ref, win_ref, wout_ref,
    acts_ref, dpre_ref, dres_ref, res_ref, pair_ref, col_ref, relay_ref,
    gin_ref, gout_ref, gin2_ref, gout2_ref, ginx_ref, goutx_ref,
    dh_ref, dhall_ref, dqkv_ref, partall_ref, gqkv_ref, gqkvall_ref, gwoall_ref,
    line_ref, smalls_ref, smallsall_ref, dense_ref, denseall_ref, densesum_ref, mine_ref, mineall_ref,
    load, pair_send, pair_recv, leg_send, leg_recv, send, recv, local,
):
    f, c, r = lax.axis_index("fsdp"), lax.axis_index("expert"), lax.axis_index("replica")
    z, y = f // 4, lax.rem(f, 4)
    other = 1 - c
    me = r * 2 + c
    sibling = {"expert": other}
    in_all = lambda p: {"replica": p // 2, "expert": lax.rem(p, 2)}
    x_ref, norm_ref = acts_ref.at[0, pl.ds(0, LEN)], acts_ref.at[0, pl.ds(LEN, LEN)]
    wo_ref = acts_ref.at[1, pl.ds(0, HW)]
    wo_mine = wo_hbm.at[pl.ds(pl.multiple_of(z * HW, HW), HW)]
    late = [
        pltpu.make_async_copy(src, dst, load.at[k])
        for k, (src, dst) in enumerate(
            zip(
                (w_hbm, att_hbm, probs_hbm, qkv_hbm, x_hbm, norm_hbm, wo_mine),
                (w_ref, att_ref, probs_ref, qkv_ref, x_ref, norm_ref, wo_ref),
            )
        )
    ]
    now = [
        pltpu.make_async_copy(src, dst, load.at[10 + k])
        for k, (src, dst) in enumerate(
            zip((two_hbm, win_hbm, g_hbm, wout_hbm), (two_ref, win_ref, g_ref, wout_ref))
        )
    ]
    for copy in now + late[:4]:
        copy.start()
    barrier = pltpu.get_barrier_semaphore()

    def greet(step, carry):
        where = {"fsdp": fsdp_peer(step, f)}
        pl.semaphore_signal(barrier, inc=1, device_id=where, device_id_type=MESH)
        return carry

    def greet_all(step, carry):
        where = in_all(lax.rem(me + step, 8))
        pl.semaphore_signal(barrier, inc=1, device_id=where, device_id_type=MESH)
        return carry

    lax.fori_loop(1, FSDP, greet, 0)
    lax.fori_loop(1, 8, greet_all, 0)
    pl.semaphore_wait(barrier, FSDP - 1 + 7)

    kinds = {
        "fsdp": (FSDP, f, fsdp_peer, lambda p: {"fsdp": p}),
        "all": (8, me, lambda step, own: lax.rem(own + step, 8), in_all),
        "row": (4, y, lambda step, own: lax.rem(own + step, 4), lambda p: {"fsdp": z * 4 + p}),
        "col": (4, z, lambda step, own: lax.rem(own + step, 4), lambda p: {"fsdp": p * 4 + y}),
        "copies": (4, r, lambda step, own: lax.rem(own + step, 4), lambda p: {"replica": p}),
    }

    def share(k, kind, block, out):
        size, own, peer, where = kinds[kind]

        def make(p, slot):
            return pltpu.make_async_remote_copy(
                src_ref=block(p), dst_ref=out.at[slot], send_sem=send.at[k, p], recv_sem=recv.at[k, slot],
                device_id=where(p), device_id_type=MESH,
            )

        def push(step, carry):
            make(peer(step, own), own).start()
            return carry

        def finish(step, carry):
            p = peer(step, own)
            copy = make(p, p)
            copy.wait_recv()
            copy.wait_send()
            return carry

        lax.fori_loop(1, size, push, 0)
        mine = pltpu.make_async_copy(block(own), out.at[own], local.at[k])
        mine.start()

        def wait():
            lax.fori_loop(1, size, finish, 0)
            mine.wait()

        return wait

    after, before, across = lax.rem(z + 1, 4), lax.rem(z + 3, 4), lax.rem(z + 2, 4)

    def home(side, block):
        half_of = lambda ref, half: ref.at[pl.ds(half * (ROWS // 2), ROWS // 2)]

        def make(p, slot):
            return pltpu.make_async_remote_copy(
                src_ref=block(p), dst_ref=col_ref.at[side, slot], send_sem=send.at[2 + side, p],
                recv_sem=recv.at[2 + side, slot], device_id={"fsdp": p * 4 + y}, device_id_type=MESH,
            )

        def first_leg(half, p):
            return pltpu.make_async_remote_copy(
                src_ref=half_of(block(across), half), dst_ref=relay_ref.at[side, half],
                send_sem=leg_send.at[side, 0, half], recv_sem=leg_recv.at[side, 0, half],
                device_id={"fsdp": p * 4 + y}, device_id_type=MESH,
            )

        def second_leg(half, slot, p):
            return pltpu.make_async_remote_copy(
                src_ref=relay_ref.at[side, half], dst_ref=half_of(col_ref.at[side, slot], half),
                send_sem=leg_send.at[side, 1, half], recv_sem=leg_recv.at[side, 1, half],
                device_id={"fsdp": p * 4 + y}, device_id_type=MESH,
            )

        first_leg(0, after).start()
        first_leg(1, before).start()
        mine = pltpu.make_async_copy(block(z), col_ref.at[side, z], local.at[2 + side])

        def whole():
            make(after, z).start()
            make(before, z).start()
            mine.start()

        def hand():
            first_leg(0, before).wait_recv()
            second_leg(0, before, after).start()
            first_leg(1, after).wait_recv()
            second_leg(1, after, before).start()

        def wait():
            for p in (after, before):
                make(p, p).wait_recv()
                make(p, p).wait_send()
            for half, p in enumerate((after, before)):
                second_leg(half, across, p).wait_recv()
                first_leg(half, p).wait_send()
                second_leg(half, across, p).wait_send()
            mine.wait()

        return whole, hand, wait

    for copy in now:
        copy.wait()
    w_in = [win_ref[:, e].reshape(D, D) for e in range(2)]
    w_out = [wout_ref[:, e].reshape(D, D) for e in range(2)]
    zero = jnp.zeros((), F32)

    def pass_on(core, chunk, side):
        rows = pl.ds(pl.multiple_of(chunk * CHUNK, CHUNK), CHUNK)
        source = pl.ds(pl.multiple_of(core * HALF + chunk * CHUNK, CHUNK), CHUNK)
        return pltpu.make_async_remote_copy(
            src_ref=res_ref.at[side, source], dst_ref=pair_ref.at[side, rows],
            send_sem=pair_send.at[side, chunk], recv_sem=pair_recv.at[side, chunk],
            device_id=sibling, device_id_type=MESH,
        )

    def expert_rows(core, step):
        rows = pl.ds(pl.multiple_of(core * HALF + step * STEP, STEP), STEP)
        x = two_ref[rows, :]
        gates, ids = [], []
        for part in range(STEP // ROWS):
            wide = jnp.concatenate(
                [facts_ref[core * 4 + step * (STEP // ROWS) + part], jnp.zeros((ROWS - 8, ROWS), F32)], axis=0
            ).T
            gates.append(wide[:, 0:1])
            ids.append(wide[:, 1:2])
        gate = jnp.concatenate(gates, axis=0)
        ids = jnp.concatenate(ids, axis=0).astype(jnp.int32) - 2 * c
        d_result = (gate * g_ref[rows, :].astype(F32)).astype(BF16)
        dres_ref[rows, :] = d_result
        is_one = ids == 1
        pre = jnp.where(is_one, dot_last(x, w_in[1]), dot_last(x, w_in[0]))
        acts, slope = gelu_pair(pre)
        d_pre = jnp.where(is_one, dot_last(d_result, w_out[1]), dot_last(d_result, w_out[0])) * slope
        total, back = 0.0, 0.0
        for e in range(2):
            here = ids == e
            acts_e = jnp.where(here, acts, zero).astype(BF16)
            d_pre_e = jnp.where(here, d_pre, zero).astype(BF16)
            acts_ref[e, rows, :] = acts_e
            dpre_ref[e, rows, :] = d_pre_e
            total += dot(acts_e, w_out[e])
            back += dot(d_pre_e, w_in[e])
        res_ref[0, rows, :] = total.astype(BF16)
        res_ref[1, rows, :] = back.astype(BF16)

    def first_rows(step, carry):
        expert_rows(other, step)
        for side in range(2):
            for part in range(STEP // CHUNK):
                pass_on(other, step * (STEP // CHUNK) + part, side).start()
        return carry

    def own_rows(step, carry):
        expert_rows(c, step)
        return carry

    lax.fori_loop(0, HALF // STEP, first_rows, 0)
    lax.fori_loop(0, HALF // STEP, own_rows, 0)
    def arrived(chunk, carry):
        for side in range(2):
            pass_on(other, chunk, side).wait_send()
            pass_on(c, chunk, side).wait_recv()
        return carry

    waits = []
    lax.fori_loop(0, HALF // CHUNK, arrived, 0)
    own_half = pl.ds(pl.multiple_of(c * HALF, HALF), HALF)
    for side in range(2):
        pair_ref[side] += res_ref[side, own_half, :]
        block = lambda p, side=side: pair_ref.at[side, pl.ds(pl.multiple_of(p * ROWS, ROWS), ROWS)]
        waits.append(home(side, block))
    for whole, _, _ in waits:
        whole()
    for e in range(2):
        g_in = dot_rows(dpre_ref[e], two_ref[...]).astype(BF16)
        for p in range(4):
            for q in range(4):
                start = p * UNITS + q * 48
                gin_ref[p, q, e] = g_in[start : start + 48]
    wait_gin = share(0, "row", lambda p: gin_ref.at[p], gin1_ref)
    for e in range(2):
        g_out = dot_rows(acts_ref[e], dres_ref[...]).astype(BF16)
        for p in range(4):
            for q in range(4):
                start = p * UNITS + q * 48
                gout_ref[q, p, e] = g_out[start : start + 48]
    for copy in late[4:]:
        copy.start()
    wait_gout = share(1, "copies", lambda p: gout_ref.at[p], gout1_ref)
    for _, hand, _ in waits:
        hand()

    upstream = own_g[...].astype(F32)
    hidden = hidden_in[...]
    rows = rows_in[...]
    router_probs = router_in[...]
    lane = lax.broadcasted_iota(jnp.int32, (ROWS, 16), 1)
    chosen = (lane == row_to_column(ids_in[...]) + 2).astype(F32)
    gate = jnp.sum(router_probs * chosen, axis=-1, keepdims=True)
    scale = rms_scale(hidden)
    gain_two = rows[1:2]
    normed = (hidden * scale * gain_two).astype(BF16).astype(F32)
    waits[0][2]()
    result = jnp.sum(col_ref[0].astype(F32), axis=0).astype(BF16).astype(F32)
    d_gate = jnp.sum(upstream * result, axis=-1, keepdims=True)
    d_logits = router_probs * (chosen * d_gate - gate * d_gate)
    d_two = jnp.dot(d_logits, rows, precision=precise, preferred_element_type=F32)
    waits[1][2]()
    d_two += jnp.sum(col_ref[1].astype(F32), axis=0).astype(BF16).astype(F32)
    d_hidden = upstream + norm_back(hidden, scale, gain_two, d_two)
    dh_ref[...] = d_hidden.astype(BF16).reshape(SEQS, SHARD, D)
    wait_dh = share(4, "fsdp", lambda p: dh_ref.at[lax.rem(p, 4)], dhall_ref)
    mixed_ref[...] = (hidden + gate * result).astype(BF16)
    g_gain_two = jnp.sum(d_two * hidden * scale, axis=0, keepdims=True)
    g_router = lax.dot_general(
        d_logits, normed, (((0,), (0,)), ((), ())), precision=precise, preferred_element_type=F32
    )

    wait_gin()
    load_gin = pltpu.make_async_copy(gin1_ref, gin_ref, load.at[8])
    load_gin.start()
    wait_gout()
    load_gout = pltpu.make_async_copy(gout1_ref, gout_ref, load.at[9])
    load_gout.start()
    load_gin.wait()
    gin2_ref[...] = jnp.sum(gin_ref[...].astype(F32), axis=0).astype(BF16)
    wait_gin2 = share(9, "copies", lambda p: gin2_ref.at[p], ginx_ref)
    load_gout.wait()
    gout2_ref[...] = jnp.sum(gout_ref[...].astype(F32), axis=0).astype(BF16)
    wait_gout2 = share(10, "row", lambda p: gout2_ref.at[p], goutx_ref)

    for copy in late:
        copy.wait()
    wait_dh()
    dh = dhall_ref[...].reshape(LEN, D)
    d_att = dot_last(dh, wo_ref[...]).astype(BF16)
    dpre_ref[1, :HW] = dot_rows(att_ref[...].reshape(LEN, HW), dh).astype(BF16)
    gwo_of = lambda p: dpre_ref.at[1, pl.ds(pl.multiple_of(p * 48, 48), 48)]
    wait_gwo = share(5, "row", gwo_of, gwoall_ref)
    line_ref[...] = jnp.zeros_like(line_ref)
    flip = lax.broadcasted_iota(jnp.int32, (LEN, LEN), 0) + lax.broadcasted_iota(jnp.int32, (LEN, LEN), 1)
    flip = (flip == LEN - 1).astype(BF16)
    for h in range(HG):
        query = qkv_ref[:, h * HD : (h + 1) * HD]
        key = qkv_ref[:, HW + h * HD : HW + (h + 1) * HD]
        value = qkv_ref[:, 2 * HW + h * HD : 2 * HW + (h + 1) * HD]
        d_head = d_att[:, h * HD : (h + 1) * HD]
        probs = probs_ref[h]
        d_probs = dot_last(d_head, value)
        inner = jnp.sum(d_probs * probs, axis=-1, keepdims=True)
        d_scores = (probs * (d_probs - inner)).astype(BF16)
        dqkv_ref[:, h * HD : (h + 1) * HD] = dot(d_scores, key).astype(BF16)
        dqkv_ref[:, HW + h * HD : HW + (h + 1) * HD] = dot_rows(d_scores, query).astype(BF16)
        dqkv_ref[:, 2 * HW + h * HD : 2 * HW + (h + 1) * HD] = dot_rows(
            probs.astype(BF16), d_head
        ).astype(BF16)
        turned = dot(flip, d_scores)
        wide = jnp.concatenate([turned, jnp.zeros((LEN, LEN), F32)], axis=1)
        wide = pltpu.roll(wide, LEN + 1, 1, stride=1, stride_axis=0)
        line_ref[pl.ds(z * HG + h, 1), :] = jnp.sum(wide, axis=0, keepdims=True)
    dqkv = dqkv_ref[...]
    gqkv_ref[...] = dot_rows(norm_ref[...], dqkv).astype(BF16).reshape(FSDP, 48, 3 * HW)
    wait_gqkv = share(6, "fsdp", lambda p: gqkv_ref.at[p], gqkvall_ref)
    part = dot_last(dqkv, w_ref[...].reshape(D, 3 * HW))
    dpre_ref[0, :LEN] = part.astype(BF16)
    part_of = lambda p: dpre_ref.at[0, pl.ds(pl.multiple_of(p * SHARD, SHARD), SHARD)]
    wait_part = share(7, "fsdp", part_of, partall_ref)
    wait_gin2()
    gin2_ref[0] = jnp.sum(ginx_ref[...].astype(F32), axis=0).astype(BF16)
    wait_gin3 = share(13, "copies", lambda p: gin2_ref.at[0], gin3_ref)
    wait_gout2()
    gout2_ref[0] = jnp.sum(goutx_ref[...].astype(F32), axis=0).astype(BF16)
    wait_gout3 = share(14, "copies", lambda p: gout2_ref.at[0], gout3_ref)
    x = x_ref[...].astype(F32)
    g_gain_one = jnp.sum(part * x * rms_scale(x), axis=0, keepdims=True)
    index = lax.broadcasted_iota(jnp.int32, (8, D), 0)
    small = jnp.where(index == 0, g_gain_one, jnp.where(index == 1, g_gain_two, 0.0))
    small = jnp.where((index >= 2) & (index < 2 + EXPERTS), g_router[:8], small)
    column = lax.broadcasted_iota(jnp.int32, (FSDP, 8, D), 2)
    first = lax.broadcasted_iota(jnp.int32, (FSDP, 8, D), 0) * 48
    small = jnp.where((column >= first) & (column < first + 48), small[None], 0.0).reshape(FSDP * 8, D)
    smalls = lax.dot_general(
        small, place_ref[...], (((1,), (1,)), ((), ())), precision=precise, preferred_element_type=F32
    ) + lax.dot_general(
        bucket_ref[...], line_ref[...], (((1,), (1,)), ((), ())), precision=precise, preferred_element_type=F32
    )
    smalls_ref[...] = smalls.reshape(FSDP, 8, 128)
    wait_smalls = share(8, "fsdp", lambda p: smalls_ref.at[p], smallsall_ref)

    wait_gwo()
    g_wo = jnp.sum(gwoall_ref[...].astype(F32), axis=0).astype(BF16)
    wait_gqkv()
    for h in range(4):
        total = jnp.sum(gqkvall_ref[4 * h : 4 * h + 4].astype(F32), axis=0).astype(BF16)
        dense_ref[h] = total[:, : 2 * HW]
        dense_ref[4 + h, :, :HW] = total[:, 2 * HW :]
        dense_ref[4 + h, :, HW:] = g_wo[:, h * HW : (h + 1) * HW]
    wait_dense = share(11, "all", lambda p: dense_ref.at[p], denseall_ref)
    wait_smalls()
    mine_ref[...] = jnp.sum(smallsall_ref[...], axis=0)
    wait_mine = share(12, "all", lambda p: mine_ref, mineall_ref)
    wait_part()
    d_one = jnp.concatenate(
        [
            sum(partall_ref[4 * h + s].astype(F32) for h in range(4))
            for s in range(SEQS)
        ],
        axis=0,
    )
    inputs = own_x[...].astype(F32)
    gtokens_ref[...] = d_hidden + norm_back(inputs, rms_scale(inputs), rows[0:1], d_one)
    wait_dense()
    densesum_ref[...] = jnp.sum(denseall_ref[...].astype(F32), axis=0).astype(BF16)
    wait_dense2 = share(15, "all", lambda p: densesum_ref, dense_out)
    wait_mine()
    totals_out[...] = jnp.sum(mineall_ref[...], axis=0)
    wait_gin3()
    wait_gout3()
    wait_dense2()


def back(*arrays):
    vmem, anywhere = pl.BlockSpec(memory_space=pltpu.VMEM), pl.BlockSpec(memory_space=pl.ANY)
    shape, buffer = jax.ShapeDtypeStruct, pltpu.VMEM
    total = 2 * HALF
    return pl.pallas_call(
        back_kernel,
        out_shape=(
            shape((ROWS, D), BF16),
            shape((ROWS, D), F32),
            shape((8, 48, 2 * HW), BF16),
            shape((8, 128), F32),
            shape((4, 2, 48, D), BF16),
            shape((4, 2, 48, D), BF16),
            shape((4, 4, 2, 48, D), BF16),
            shape((4, 4, 2, 48, D), BF16),
        ),
        in_specs=[vmem] * 9 + [anywhere] * 11,
        out_specs=(vmem,) * 6 + (anywhere,) * 2,
        scratch_shapes=[buffer(array.shape, array.dtype) for array in arrays[12:]]
        + [
            buffer((2, total, D), BF16),
            buffer((2, total, D), BF16),
            buffer((total, D), BF16),
            buffer((2, total, D), BF16),
            buffer((2, HALF, D), BF16),
            buffer((2, 4, ROWS, D), BF16),
            buffer((2, 2, ROWS // 2, D), BF16),
            buffer((4, 4, 2, 48, D), BF16),
            buffer((4, 4, 2, 48, D), BF16),
            buffer((4, 2, 48, D), BF16),
            buffer((4, 2, 48, D), BF16),
            buffer((4, 2, 48, D), BF16),
            buffer((4, 2, 48, D), BF16),
            buffer((SEQS, SHARD, D), BF16),
            buffer((FSDP, SHARD, D), BF16),
            buffer((LEN, 3 * HW), BF16),
            buffer((FSDP, SHARD, D), BF16),
            buffer((FSDP, 48, 3 * HW), BF16),
            buffer((FSDP, 48, 3 * HW), BF16),
            buffer((4, 48, D), BF16),
            buffer((128, 2 * LEN), F32),
            buffer((FSDP, 8, 128), F32),
            buffer((FSDP, 8, 128), F32),
            buffer((8, 48, 2 * HW), BF16),
            buffer((8, 48, 2 * HW), BF16),
            buffer((48, 2 * HW), BF16),
            buffer((8, 128), F32),
            buffer((8, 8, 128), F32),
            pltpu.SemaphoreType.DMA((14,)),
            pltpu.SemaphoreType.DMA((2, HALF // CHUNK)),
            pltpu.SemaphoreType.DMA((2, HALF // CHUNK)),
            pltpu.SemaphoreType.DMA((2, 2, 2)),
            pltpu.SemaphoreType.DMA((2, 2, 2)),
            pltpu.SemaphoreType.DMA((16, 16)),
            pltpu.SemaphoreType.DMA((16, 16)),
            pltpu.SemaphoreType.DMA((16,)),
        ],
        compiler_params=pltpu.CompilerParams(
            collective_id=1, has_side_effects=True, vmem_limit_bytes=VMEM_BYTES
        ),
        name="back",
    )(*arrays)


def finish_kernel(
    mixed_ref, tokens_ref, dense_ref, totals_ref, gin_ref, gout_ref,
    mixed_out, tokens_out, gain_one_out, gq_out, gk_out, gv_out, go_out, gbias_out, gain_two_out, router_out,
    gin_out, gout_out,
):
    mixed_out[...] = mixed_ref[...]
    tokens_out[...] = tokens_ref[...]
    totals = totals_ref[...]
    gain_one_out[...] = totals[0:1, :48]
    gain_two_out[...] = totals[1:2, :48]
    router_out[...] = totals[2 : 2 + EXPERTS, :48]
    gbias_out[...] = totals[6:8, :HEADS]
    for h in range(4):
        at = slice(h * HW, (h + 1) * HW)
        first, second = dense_ref[h].astype(F32), dense_ref[4 + h].astype(F32)
        gq_out[:, at], gk_out[:, at] = first[:, :HW], first[:, HW:]
        gv_out[:, at], go_out[:, at] = second[:, :HW], second[:, HW:]
    for q in range(4):
        at = slice(q * 48, (q + 1) * 48)
        gin_out[:, at, :] = gin_ref[q].astype(F32)
        gout_out[:, at, :] = gout_ref[q].astype(F32)


def finish(*arrays):
    vmem, shape = pl.BlockSpec(memory_space=pltpu.VMEM), jax.ShapeDtypeStruct
    return pl.pallas_call(
        finish_kernel,
        out_shape=(
            shape((ROWS, D), BF16),
            shape((ROWS, D), F32),
            shape((1, 48), F32),
            shape((48, D), F32),
            shape((48, D), F32),
            shape((48, D), F32),
            shape((48, D), F32),
            shape((2, HEADS), F32),
            shape((1, 48), F32),
            shape((EXPERTS, 48), F32),
            shape((2, UNITS, D), F32),
            shape((2, UNITS, D), F32),
        ),
        in_specs=[vmem] * 6,
        out_specs=(vmem,) * 12,
        compiler_params=pltpu.CompilerParams(vmem_limit_bytes=32 * 1024 * 1024),
        name="finish",
    )(*arrays)


def body(
    tokens, lengths, expert_ids, gain_attn, w_query, w_key, w_value, w_output, rel_bias, gain_ffn,
    router, expert_in, expert_out, out_grad,
):
    onehot = bucket_rows()
    tokens, out_grad = tokens[0], out_grad[0].reshape(ROWS, D)
    place = np.zeros((128, D), np.float32)
    place[np.arange(D) % 48, np.arange(D)] = 1.0
    buckets = np.zeros((FSDP, 16, 2 * LEN), np.float32)
    buckets[:, 6:8] = onehot.T.reshape(FSDP, 2, 2 * LEN)
    inputs = tokens.reshape(ROWS, D)
    ids = expert_ids.reshape(1, ROWS)
    (
        x_seq, w_packed, wo_full, normed_one, qkv, attended, probs, hidden_one, router_probs, rows,
        two_all, g_all, facts_all, win_all, wout_all,
    ) = front(
        lengths, ids, jnp.asarray(place), jnp.asarray(buckets.reshape(FSDP * 16, 2 * LEN)),
        inputs, gain_attn.reshape(1, 48), gain_ffn.reshape(1, 48), router.T, rel_bias, w_query, w_key, w_value,
        tokens, w_output, out_grad, expert_in, expert_out,
    )
    backs = np.zeros((FSDP, 8, 2 * LEN), np.float32)
    backs[:, 6:8] = onehot.T.reshape(FSDP, 2, 2 * LEN)
    *parts, _, _ = back(
        facts_all, hidden_one, router_probs, rows, inputs, out_grad, ids,
        jnp.asarray(place), jnp.asarray(backs.reshape(FSDP * 8, 2 * LEN)),
        x_seq.reshape(LEN, D), normed_one, wo_full.reshape(D, D), w_packed, attended, probs, qkv,
        two_all.reshape(8 * ROWS, D), g_all.reshape(8 * ROWS, D), win_all, wout_all,
    )
    mixed, grad_tokens, gain_one, gq, gk, gv, go, bias, gain_two, routing, gin, gout = finish(*parts)
    return (
        mixed.reshape(1, SEQS, SHARD, D),
        grad_tokens.reshape(1, SEQS, SHARD, D),
        gain_one.reshape(48),
        gq,
        gk,
        gv,
        go,
        bias,
        gain_two.reshape(48),
        routing.T,
        gin,
        gout,
    )


def solution(mesh):
    in_specs = (
        P(("replica", "expert"), None, "fsdp", None),
        P(("replica", "expert"), None),
        P(("replica", "expert", "fsdp"), None, None),
        P("fsdp"),
        P("fsdp", None),
        P("fsdp", None),
        P("fsdp", None),
        P("fsdp", None),
        P("fsdp", None),
        P("fsdp"),
        P("fsdp", None),
        P("expert", "fsdp", None),
        P("expert", "fsdp", None),
        P(("replica", "expert"), None, "fsdp", None),
    )
    out_specs = (
        P(("replica", "expert"), None, "fsdp", None),
        P(("replica", "expert"), None, "fsdp", None),
        P("fsdp"),
        P("fsdp", None),
        P("fsdp", None),
        P("fsdp", None),
        P("fsdp", None),
        P("fsdp", None),
        P("fsdp"),
        P("fsdp", None),
        P("expert", "fsdp", None),
        P("expert", "fsdp", None),
    )
    return jax.shard_map(body, mesh=mesh, in_specs=in_specs, out_specs=out_specs, check_vma=False)
```

```python
import functools
import math

import jax
import jax.numpy as jnp
import numpy as np
from jax import lax
from jax.experimental import pallas as pl
from jax.experimental.pallas import tpu as pltpu
from jax.sharding import PartitionSpec as P

MAXDIST = 128
MESH = pl.DeviceIdType.MESH
F32, BF16 = jnp.float32, jnp.bfloat16
precise = lax.Precision.HIGHEST
VMEM_BYTES = 60 * 1024 * 1024

D, HEADS, HD, FF, NB, LEN, SEQS, SHARD, ROWS = 768, 12, 64, 3072, 32, 512, 4, 32, 128
EXPERTS, FSDP, UNITS = 4, 16, 192
HG = 3
HW = HG * HD


def bucket_of(offset):
    per_side, exact = NB // 2, NB // 4
    dist = abs(offset)
    if dist < exact:
        near = dist
    else:
        near = exact + int(math.log(dist / exact) / math.log(MAXDIST / exact) * (per_side - exact))
        near = min(near, per_side - 1)
    return (per_side if offset > 0 else 0) + near


def bucket_rows():
    onehot = np.zeros((2 * LEN, NB), np.float32)
    for index in range(2 * LEN):
        offset = index if index < LEN else index - 2 * LEN
        if offset != -LEN:
            onehot[index, bucket_of(offset)] = 1.0
    return onehot


def fsdp_peer(step, me):
    row = lax.rem(me // 4 + step // 4, 4)
    col = lax.rem(lax.rem(me, 4) + lax.rem(step, 4), 4)
    return row * 4 + col


def dot(left, right):
    return jnp.dot(left, right, preferred_element_type=F32)


def dot_rows(left, right):
    return lax.dot_general(left, right, (((0,), (0,)), ((), ())), preferred_element_type=F32)


def dot_last(left, right):
    return lax.dot_general(left, right, (((1,), (1,)), ((), ())), preferred_element_type=F32)


def gelu_pair(pre):
    cdf = 0.5 * (1.0 + lax.erf(pre * (2.0**-0.5)))
    pdf = jnp.exp(-0.5 * pre * pre) * (1.0 / math.sqrt(2.0 * math.pi))
    return pre * cdf, cdf + pre * pdf


def attention_forward(x_ref, gain, w_ref, bias_ref, bias_row, length, att_ref, probs_ref, qkv_ref, norm_ref):
    x = x_ref[...].reshape(LEN, D).astype(F32)
    scale = lax.rsqrt(jnp.mean(x * x, axis=-1, keepdims=True) + 1e-6)
    normed = (x * scale * gain).astype(BF16)
    norm_ref[...] = normed
    qkv_ref[...] = dot(normed, w_ref[...].reshape(D, 3 * HW)).astype(BF16)
    live = lax.broadcasted_iota(jnp.int32, (LEN, LEN), 1) < length
    for h in range(HG):
        query = qkv_ref[:, h * HD : (h + 1) * HD]
        key = qkv_ref[:, HW + h * HD : HW + (h + 1) * HD]
        value = qkv_ref[:, 2 * HW + h * HD : 2 * HW + (h + 1) * HD]
        line = jnp.broadcast_to(bias_ref[pl.ds(bias_row + h, 1), :], (LEN, 2 * LEN))
        bias = pltpu.roll(line, 0, 1, stride=1, stride_axis=0)[:, :LEN]
        scores = jnp.where(live, dot_last(query, key) + bias, -1e30)
        powers = jnp.exp(scores - jnp.max(scores, axis=-1, keepdims=True))
        probs = powers / jnp.sum(powers, axis=-1, keepdims=True)
        probs_ref[h] = probs
        att = dot(probs.astype(BF16), value).astype(BF16)
        att_ref[:, :, h * HD : (h + 1) * HD] = att.reshape(FSDP, SHARD, HD)


def unpack(small, place):
    wide = dot(small, place).reshape(FSDP, 16, D)
    owner = lax.broadcasted_iota(jnp.int32, (FSDP, 16, D), 2)
    first = lax.broadcasted_iota(jnp.int32, (FSDP, 16, D), 0) * 48
    return jnp.sum(jnp.where((owner >= first) & (owner < first + 48), wide, 0.0), axis=0)


def row_to_column(row):
    return jnp.broadcast_to(row.astype(F32), (ROWS, ROWS)).T[:, :1].astype(jnp.int32)


def front_kernel(
    length_ref, ids_ref, place_ref, bucket_ref, own_x_ref,
    gain_one_ref, gain_two_ref, router_in, bias_in, wq_ref, wk_ref, wv_ref,
    tokens, w_output, out_grad, ein, eout,
    x_out, w_out, wo_out, norm_out, qkv_out, att_out, probs_out, hidden_ref, router_ref, rows_ref,
    two_all, g_all, facts_all, win_all, wout_all,
    x_ref, w_ref, wo_ref, norm_ref, qkv_ref, att_ref, probs_ref, save,
    packed, small, small_ref, back_ref, bias_ref, two_ref, facts_ref,
    send, recv, local, pass_send, pass_recv, cross_send, cross_recv, relay_send, relay_recv,
):
    f, c, r = lax.axis_index("fsdp"), lax.axis_index("expert"), lax.axis_index("replica")
    z, y = f // 4, lax.rem(f, 4)
    other = 1 - c
    sibling = {"expert": other}
    in_col = lambda p: {"fsdp": p * 4 + y}
    in_row = lambda p: {"fsdp": z * 4 + p}
    barrier = pltpu.get_barrier_semaphore()

    def greet(where):
        pl.semaphore_signal(barrier, inc=1, device_id=where, device_id_type=MESH)

    def hello(step, carry):
        greet({"fsdp": fsdp_peer(step, f)})
        return carry

    lax.fori_loop(1, FSDP, hello, 0)
    greet(sibling)
    for step in range(1, 4):
        greet({"fsdp": lax.rem(z + step, 4) * 4 + y, "expert": other})
        greet({"replica": lax.rem(r + step, 4)})
    for h in range(4):
        for side, weight in enumerate((wq_ref, wk_ref, wv_ref)):
            packed[h, :, side * HW : (side + 1) * HW] = weight[:, h * HW : (h + 1) * HW]
    unit = lambda rows: (
        lax.broadcasted_iota(jnp.int32, (rows, 128), 0) == lax.broadcasted_iota(jnp.int32, (rows, 128), 1)
    ).astype(BF16)
    shift = lambda rows, by: (
        lax.broadcasted_iota(jnp.int32, (rows, 16), 0) + by == lax.broadcasted_iota(jnp.int32, (rows, 16), 1)
    ).astype(BF16)
    index = lax.broadcasted_iota(jnp.int32, (16, 128), 0)
    lines = dot_rows(shift(EXPERTS, 2), dot(router_in[...], unit(48)).astype(BF16))
    lines += dot_rows(shift(2, 6), dot(bias_in[...], unit(HEADS)).astype(BF16))
    lines += jnp.where(index == 0, dot(gain_one_ref[...], unit(48)), 0.0)
    lines += jnp.where(index == 1, dot(gain_two_ref[...], unit(48)), 0.0)
    small[...] = lines.astype(BF16)
    pl.semaphore_wait(barrier, FSDP - 1 + 7)

    def remote(k, src, dst, p, slot, where):
        return pltpu.make_async_remote_copy(
            src_ref=src, dst_ref=dst, send_sem=send.at[k, p], recv_sem=recv.at[k, slot],
            device_id=where, device_id_type=MESH,
        )

    def everyone(k, block, out):
        make = lambda p, slot: remote(k, block(p), out.at[slot], p, slot, {"fsdp": p})

        def push(step, carry):
            make(fsdp_peer(step, f), f).start()
            return carry

        def finish(step, carry):
            p = fsdp_peer(step, f)
            copy = make(p, p)
            copy.wait_recv()
            copy.wait_send()
            return carry

        own = pltpu.make_async_copy(block(f), out.at[f], local.at[k])
        lax.fori_loop(1, FSDP, push, 0)
        own.start()

        def wait():
            lax.fori_loop(1, FSDP, finish, 0)
            own.wait()

        return wait

    def ring(k, relay_k, src, out, me, where, cut, passed=lambda block, half: None):
        after, before, across = lax.rem(me + 1, 4), lax.rem(me + 3, 4), lax.rem(me + 2, 4)
        make = lambda p, slot: remote(k, src, out.at[slot], p, slot, where(p))

        def hand(block, half, p):
            there = cut(out.at[block], half)
            return pltpu.make_async_remote_copy(
                src_ref=there, dst_ref=there, send_sem=relay_send.at[relay_k, half],
                recv_sem=relay_recv.at[relay_k, half], device_id=where(p), device_id_type=MESH,
            )

        make(after, me).start()
        make(before, me).start()
        own = pltpu.make_async_copy(src, out.at[me], local.at[k])
        own.start()

        def relay():
            make(before, before).wait_recv()
            hand(before, 0, after).start()
            make(after, after).wait_recv()
            hand(after, 1, before).start()
            for block in (before, after):
                for half in range(2):
                    passed(block, half)

        def wait():
            for half, p in enumerate((after, before)):
                hand(across, half, p).wait_recv()
                passed(across, half)
            make(after, after).wait_send()
            make(before, before).wait_send()
            hand(before, 0, after).wait_send()
            hand(after, 1, before).wait_send()
            own.wait()

        return relay, wait

    def column(k, pass_k, src, out):
        def to_sibling(core, block, half, source=None):
            rows = pl.ds(half * (ROWS // 2), ROWS // 2)
            there = out.at[core * 4 + block, rows]
            return pltpu.make_async_remote_copy(
                src_ref=there if source is None else source.at[rows], dst_ref=there,
                send_sem=pass_send.at[pass_k, block, half], recv_sem=pass_recv.at[pass_k, block, half],
                device_id=sibling, device_id_type=MESH,
            )

        cut = lambda ref, half: ref.at[pl.ds(half * (ROWS // 2), ROWS // 2)]
        passed = lambda block, half: to_sibling(c, block, half).start()
        relay, wait_own = ring(k, pass_k, src, out.at[pl.ds(c * 4, 4)], z, in_col, cut, passed)
        for half in range(2):
            to_sibling(c, z, half, src).start()

        def wait():
            wait_own()
            for block in range(4):
                for half in range(2):
                    to_sibling(c, block, half).wait_send()
                    to_sibling(other, block, half).wait_recv()

        return relay, wait

    wait_x = everyone(0, lambda p: tokens.at[lax.rem(p, 4)], x_ref)
    wait_small = everyone(1, lambda p: small, small_ref)
    wait_w = everyone(2, lambda p: packed.at[p // 4], w_ref)
    quarter = pl.ds(pl.multiple_of(r * 48, 48), 48)
    ring_steps = (1, 3, 2)

    def fetch(p, slot):
        return remote(
            5, eout.at[:, quarter], wout_all.at[slot, :, quarter], p, slot, in_row(p)
        )

    def cross(block, q, part):
        rows = pl.ds(pl.multiple_of(part * 48, 48), 48)
        return pltpu.make_async_remote_copy(
            src_ref=wout_all.at[block, :, rows], dst_ref=wout_all.at[block, :, rows],
            send_sem=cross_send.at[block, q], recv_sem=cross_recv.at[block, part],
            device_id={"replica": q}, device_id_type=MESH,
        )

    for step in ring_steps:
        fetch(lax.rem(y + step, 4), y).start()
    own_wout = pltpu.make_async_copy(eout, wout_all.at[y], local.at[5])
    own_wout.start()

    def cross_all():
        for step in ring_steps:
            block = lax.rem(y + step, 4)
            fetch(block, block).wait_recv()
            for turn in ring_steps:
                cross(block, lax.rem(r + turn, 4), r).start()

    def wait_wout():
        own_wout.wait()
        for step in ring_steps:
            block = lax.rem(y + step, 4)
            fetch(block, block).wait_send()
            for turn in ring_steps:
                q = lax.rem(r + turn, 4)
                cross(block, q, r).wait_send()
                cross(block, q, q).wait_recv()


    wait_small()
    smalls = small_ref[...].reshape(FSDP * 16, 128)
    rows = unpack(smalls, place_ref[...].astype(BF16))
    rows_ref[...] = rows
    bias_ref[...] = dot_rows(smalls, bucket_ref[...].astype(BF16))[:16]
    wait_x()
    wait_w()
    wait_wo = everyone(3, lambda p: w_output, wo_ref)
    forward_g, wait_g = column(6, 0, out_grad, g_all)
    relay_win, wait_win = ring(
        4, 2, ein, win_all, y, in_row, lambda ref, half: ref.at[pl.ds(half, 1)]
    )
    cross_all()
    attention_forward(
        x_ref, rows[0:1], w_ref, bias_ref, HG * z, length_ref[0, y], att_ref, probs_ref, qkv_ref, norm_ref
    )

    wait_att = everyone(7, lambda p: att_ref.at[p], back_ref)
    pairs = (
        (x_ref, x_out), (w_ref, w_out), (norm_ref, norm_out), (qkv_ref, qkv_out), (att_ref, att_out),
        (probs_ref, probs_out), (wo_ref, wo_out),
    )
    saves = [pltpu.make_async_copy(src, dst, save.at[k]) for k, (src, dst) in enumerate(pairs)]
    forward_g()
    for copy in saves[:6]:
        copy.start()
    wait_wo()
    saves[6].start()
    wait_att()
    hidden = own_x_ref[...].astype(F32)
    for h in range(4):
        att = jnp.concatenate([back_ref[h * 4 + s] for s in range(SEQS)], axis=0)
        hidden += dot(att, wo_ref[4 * h : 4 * h + 4].reshape(HW, D))
    hidden_ref[...] = hidden
    scale = lax.rsqrt(jnp.mean(hidden * hidden, axis=-1, keepdims=True) + 1e-6)
    two = (hidden * scale * rows[1:2]).astype(BF16)
    two_ref[...] = two
    forward_two, wait_two = column(8, 1, two_ref, two_all)
    logits = lax.dot_general(
        two.astype(F32), rows, (((1,), (1,)), ((), ())), precision=precise, preferred_element_type=F32
    )
    lane = lax.broadcasted_iota(jnp.int32, (ROWS, 16), 1)
    inside = (lane >= 2) & (lane < 2 + EXPERTS)
    logits = jnp.where(inside, logits, -1e30)
    powers = jnp.where(inside, jnp.exp(logits - jnp.max(logits, axis=-1, keepdims=True)), 0.0)
    router_probs = powers / jnp.sum(powers, axis=-1, keepdims=True)
    router_ref[...] = router_probs
    ids = row_to_column(ids_ref[...])
    gate = jnp.sum(jnp.where(lane == ids + 2, router_probs, 0.0), axis=-1, keepdims=True)
    wide = lax.broadcasted_iota(jnp.int32, (ROWS, ROWS), 1)
    facts = jnp.where(wide == 0, gate, jnp.where(wide == 1, ids.astype(F32), 0.0))
    facts_ref[...] = facts.T[:8]
    me = c * 4 + z
    spots = [(other if i % 2 == 0 else c, lax.rem(z + (i + 1) // 2, 4)) for i in range(7)]
    fact = lambda core, p, slot: remote(
        9, facts_ref, facts_all.at[slot], core * 4 + p, slot, {"fsdp": p * 4 + y, "expert": core}
    )
    for core, p in spots:
        fact(core, p, me).start()
    own_facts = pltpu.make_async_copy(facts_ref, facts_all.at[me], local.at[9])
    own_facts.start()
    forward_two()
    relay_win()
    for copy in saves:
        copy.wait()
    wait_two()
    wait_g()
    wait_win()
    wait_wout()
    for core, p in spots:
        copy = fact(core, p, core * 4 + p)
        copy.wait_recv()
        copy.wait_send()
    own_facts.wait()


def front(lengths, *arrays):
    vmem, smem = pl.BlockSpec(memory_space=pltpu.VMEM), pl.BlockSpec(memory_space=pltpu.SMEM)
    anywhere = pl.BlockSpec(memory_space=pl.ANY)
    shape = jax.ShapeDtypeStruct
    return pl.pallas_call(
        front_kernel,
        out_shape=(
            shape((FSDP, SHARD, D), BF16),
            shape((FSDP, 48, 3 * HW), BF16),
            shape((FSDP, 48, D), BF16),
            shape((LEN, D), BF16),
            shape((LEN, 3 * HW), BF16),
            shape((FSDP, SHARD, HW), BF16),
            shape((HG, LEN, LEN), F32),
            shape((ROWS, D), F32),
            shape((ROWS, 16), F32),
            shape((16, D), F32),
            shape((8, ROWS, D), BF16),
            shape((8, ROWS, D), BF16),
            shape((8, 8, ROWS), F32),
            shape((4, 2, UNITS, D), BF16),
            shape((4, 2, UNITS, D), BF16),
        ),
        in_specs=[smem] + [vmem] * 11 + [anywhere] * 5,
        out_specs=(anywhere,) * 7 + (vmem,) * 3 + (anywhere,) * 5,
        scratch_shapes=[
            pltpu.VMEM((FSDP, SHARD, D), BF16),
            pltpu.VMEM((FSDP, 48, 3 * HW), BF16),
            pltpu.VMEM((FSDP, 48, D), BF16),
            pltpu.VMEM((LEN, D), BF16),
            pltpu.VMEM((LEN, 3 * HW), BF16),
            pltpu.VMEM((FSDP, SHARD, HW), BF16),
            pltpu.VMEM((HG, LEN, LEN), F32),
            pltpu.SemaphoreType.DMA((7,)),
            pltpu.VMEM((4, 48, 3 * HW), BF16),
            pltpu.VMEM((16, 128), BF16),
            pltpu.VMEM((FSDP, 16, 128), BF16),
            pltpu.VMEM((FSDP, SHARD, HW), BF16),
            pltpu.VMEM((16, 2 * LEN), F32),
            pltpu.VMEM((ROWS, D), BF16),
            pltpu.VMEM((8, ROWS), F32),
            pltpu.SemaphoreType.DMA((10, 16)),
            pltpu.SemaphoreType.DMA((10, 16)),
            pltpu.SemaphoreType.DMA((10,)),
            pltpu.SemaphoreType.DMA((2, 4, 2)),
            pltpu.SemaphoreType.DMA((2, 4, 2)),
            pltpu.SemaphoreType.DMA((4, 4)),
            pltpu.SemaphoreType.DMA((4, 4)),
            pltpu.SemaphoreType.DMA((3, 2)),
            pltpu.SemaphoreType.DMA((3, 2)),
        ],
        compiler_params=pltpu.CompilerParams(
            collective_id=0, has_side_effects=True, vmem_limit_bytes=VMEM_BYTES
        ),
        name="front",
    )(lengths, *arrays)


def rms_scale(values):
    return lax.rsqrt(jnp.mean(values * values, axis=-1, keepdims=True) + 1e-6)


def norm_back(values, scale, gain, upstream):
    weighted = upstream * gain
    inner = jnp.mean(values * weighted, axis=-1, keepdims=True)
    return scale * weighted - values * (scale * scale * scale * inner)


HALF = 4 * ROWS
STEP = 256
CHUNK = 64


def back_kernel(
    facts_ref, hidden_in, router_in, rows_in, own_x, own_g, ids_in, place_ref, bucket_ref,
    x_hbm, norm_hbm, wo_hbm, w_hbm, att_hbm, probs_hbm, qkv_hbm, two_hbm, g_hbm, win_hbm, wout_hbm,
    mixed_ref, gtokens_ref, dense_out, totals_out, gin3_ref, gout3_ref, gin1_ref, gout1_ref,
    w_ref, att_ref, probs_ref, qkv_ref, two_ref, g_ref, win_ref, wout_ref,
    acts_ref, dpre_ref, dres_ref, res_ref, pair_ref, col_ref, relay_ref,
    gin_ref, gout_ref, gin2_ref, gout2_ref, ginx_ref, goutx_ref,
    dh_ref, dhall_ref, dqkv_ref, dscores_ref, partall_ref, gqkv_ref, gqkvall_ref, gwoall_ref,
    line_ref, smalls_ref, smallsall_ref, dense_ref, denseall_ref, densesum_ref, mine_ref, mineall_ref,
    load, pair_send, pair_recv, leg_send, leg_recv, send, recv, local,
):
    f, c, r = lax.axis_index("fsdp"), lax.axis_index("expert"), lax.axis_index("replica")
    z, y = f // 4, lax.rem(f, 4)
    other = 1 - c
    me = r * 2 + c
    sibling = {"expert": other}
    in_all = lambda p: {"replica": p // 2, "expert": lax.rem(p, 2)}
    x_ref, norm_ref = acts_ref.at[0, pl.ds(0, LEN)], acts_ref.at[0, pl.ds(LEN, LEN)]
    wo_ref = acts_ref.at[1, pl.ds(0, HW)]
    wo_mine = wo_hbm.at[pl.ds(pl.multiple_of(z * HW, HW), HW)]
    late = [
        pltpu.make_async_copy(src, dst, load.at[k])
        for k, (src, dst) in enumerate(
            zip(
                (w_hbm, att_hbm, probs_hbm, qkv_hbm, x_hbm, norm_hbm, wo_mine),
                (w_ref, att_ref, probs_ref, qkv_ref, x_ref, norm_ref, wo_ref),
            )
        )
    ]
    now = [
        pltpu.make_async_copy(src, dst, load.at[10 + k])
        for k, (src, dst) in enumerate(
            zip((two_hbm, win_hbm, g_hbm, wout_hbm), (two_ref, win_ref, g_ref, wout_ref))
        )
    ]
    for copy in now + late[:4]:
        copy.start()
    barrier = pltpu.get_barrier_semaphore()

    def greet(step, carry):
        where = {"fsdp": fsdp_peer(step, f)}
        pl.semaphore_signal(barrier, inc=1, device_id=where, device_id_type=MESH)
        return carry

    def greet_all(step, carry):
        where = in_all(lax.rem(me + step, 8))
        pl.semaphore_signal(barrier, inc=1, device_id=where, device_id_type=MESH)
        return carry

    lax.fori_loop(1, FSDP, greet, 0)
    lax.fori_loop(1, 8, greet_all, 0)
    pl.semaphore_wait(barrier, FSDP - 1 + 7)

    kinds = {
        "fsdp": (FSDP, f, fsdp_peer, lambda p: {"fsdp": p}),
        "all": (8, me, lambda step, own: lax.rem(own + step, 8), in_all),
        "row": (4, y, lambda step, own: lax.rem(own + step, 4), lambda p: {"fsdp": z * 4 + p}),
        "col": (4, z, lambda step, own: lax.rem(own + step, 4), lambda p: {"fsdp": p * 4 + y}),
        "copies": (4, r, lambda step, own: lax.rem(own + step, 4), lambda p: {"replica": p}),
    }

    def share(k, kind, block, out):
        size, own, peer, where = kinds[kind]

        def make(p, slot):
            return pltpu.make_async_remote_copy(
                src_ref=block(p), dst_ref=out.at[slot], send_sem=send.at[k, p], recv_sem=recv.at[k, slot],
                device_id=where(p), device_id_type=MESH,
            )

        def push(step, carry):
            make(peer(step, own), own).start()
            return carry

        def finish(step, carry):
            p = peer(step, own)
            copy = make(p, p)
            copy.wait_recv()
            copy.wait_send()
            return carry

        lax.fori_loop(1, size, push, 0)
        mine = pltpu.make_async_copy(block(own), out.at[own], local.at[k])
        mine.start()

        def wait():
            lax.fori_loop(1, size, finish, 0)
            mine.wait()

        return wait

    after, before, across = lax.rem(z + 1, 4), lax.rem(z + 3, 4), lax.rem(z + 2, 4)

    def home(side, block):
        half_of = lambda ref, half: ref.at[pl.ds(half * (ROWS // 2), ROWS // 2)]

        def make(p, slot):
            return pltpu.make_async_remote_copy(
                src_ref=block(p), dst_ref=col_ref.at[side, slot], send_sem=send.at[2 + side, p],
                recv_sem=recv.at[2 + side, slot], device_id={"fsdp": p * 4 + y}, device_id_type=MESH,
            )

        def first_leg(half, p):
            return pltpu.make_async_remote_copy(
                src_ref=half_of(block(across), half), dst_ref=relay_ref.at[side, half],
                send_sem=leg_send.at[side, 0, half], recv_sem=leg_recv.at[side, 0, half],
                device_id={"fsdp": p * 4 + y}, device_id_type=MESH,
            )

        def second_leg(half, slot, p):
            return pltpu.make_async_remote_copy(
                src_ref=relay_ref.at[side, half], dst_ref=half_of(col_ref.at[side, slot], half),
                send_sem=leg_send.at[side, 1, half], recv_sem=leg_recv.at[side, 1, half],
                device_id={"fsdp": p * 4 + y}, device_id_type=MESH,
            )

        first_leg(0, after).start()
        first_leg(1, before).start()
        mine = pltpu.make_async_copy(block(z), col_ref.at[side, z], local.at[2 + side])

        def whole():
            make(after, z).start()
            make(before, z).start()
            mine.start()

        def hand():
            first_leg(0, before).wait_recv()
            second_leg(0, before, after).start()
            first_leg(1, after).wait_recv()
            second_leg(1, after, before).start()

        def wait():
            for p in (after, before):
                make(p, p).wait_recv()
                make(p, p).wait_send()
            for half, p in enumerate((after, before)):
                second_leg(half, across, p).wait_recv()
                first_leg(half, p).wait_send()
                second_leg(half, across, p).wait_send()
            mine.wait()

        return whole, hand, wait

    for copy in now:
        copy.wait()
    w_in = [win_ref[:, e].reshape(D, D) for e in range(2)]
    w_out = [wout_ref[:, e].reshape(D, D) for e in range(2)]
    zero = jnp.zeros((), F32)

    def pass_on(core, chunk, side):
        rows = pl.ds(pl.multiple_of(chunk * CHUNK, CHUNK), CHUNK)
        source = pl.ds(pl.multiple_of(core * HALF + chunk * CHUNK, CHUNK), CHUNK)
        return pltpu.make_async_remote_copy(
            src_ref=res_ref.at[side, source], dst_ref=pair_ref.at[side, rows],
            send_sem=pair_send.at[side, chunk], recv_sem=pair_recv.at[side, chunk],
            device_id=sibling, device_id_type=MESH,
        )

    def expert_rows(core, step):
        rows = pl.ds(pl.multiple_of(core * HALF + step * STEP, STEP), STEP)
        x = two_ref[rows, :]
        gates, ids = [], []
        for part in range(STEP // ROWS):
            wide = jnp.concatenate(
                [facts_ref[core * 4 + step * (STEP // ROWS) + part], jnp.zeros((ROWS - 8, ROWS), F32)], axis=0
            ).T
            gates.append(wide[:, 0:1])
            ids.append(wide[:, 1:2])
        gate = jnp.concatenate(gates, axis=0)
        ids = jnp.concatenate(ids, axis=0).astype(jnp.int32) - 2 * c
        d_result = (gate * g_ref[rows, :].astype(F32)).astype(BF16)
        dres_ref[rows, :] = d_result
        is_one = ids == 1
        pre = jnp.where(is_one, dot_last(x, w_in[1]), dot_last(x, w_in[0]))
        acts, slope = gelu_pair(pre)
        d_pre = jnp.where(is_one, dot_last(d_result, w_out[1]), dot_last(d_result, w_out[0])) * slope
        total, back = 0.0, 0.0
        for e in range(2):
            here = ids == e
            acts_e = jnp.where(here, acts, zero).astype(BF16)
            d_pre_e = jnp.where(here, d_pre, zero).astype(BF16)
            acts_ref[e, rows, :] = acts_e
            dpre_ref[e, rows, :] = d_pre_e
            total += dot(acts_e, w_out[e])
            back += dot(d_pre_e, w_in[e])
        res_ref[0, rows, :] = total.astype(BF16)
        res_ref[1, rows, :] = back.astype(BF16)

    def first_rows(step, carry):
        expert_rows(other, step)
        for side in range(2):
            for part in range(STEP // CHUNK):
                pass_on(other, step * (STEP // CHUNK) + part, side).start()
        return carry

    def own_rows(step, carry):
        expert_rows(c, step)
        return carry

    lax.fori_loop(0, HALF // STEP, first_rows, 0)
    lax.fori_loop(0, HALF // STEP, own_rows, 0)
    def arrived(chunk, carry):
        for side in range(2):
            pass_on(other, chunk, side).wait_send()
            pass_on(c, chunk, side).wait_recv()
        return carry

    waits = []
    lax.fori_loop(0, HALF // CHUNK, arrived, 0)
    own_half = pl.ds(pl.multiple_of(c * HALF, HALF), HALF)
    for side in range(2):
        pair_ref[side] += res_ref[side, own_half, :]
        block = lambda p, side=side: pair_ref.at[side, pl.ds(pl.multiple_of(p * ROWS, ROWS), ROWS)]
        waits.append(home(side, block))
    for whole, _, _ in waits:
        whole()
    for e in range(2):
        g_in = dot_rows(dpre_ref[e], two_ref[...]).astype(BF16)
        for p in range(4):
            for q in range(4):
                start = p * UNITS + q * 48
                gin_ref[p, q, e] = g_in[start : start + 48]
    wait_gin = share(0, "row", lambda p: gin_ref.at[p], gin1_ref)
    for e in range(2):
        g_out = dot_rows(acts_ref[e], dres_ref[...]).astype(BF16)
        for p in range(4):
            for q in range(4):
                start = p * UNITS + q * 48
                gout_ref[q, p, e] = g_out[start : start + 48]
    for copy in late[4:]:
        copy.start()
    wait_gout = share(1, "copies", lambda p: gout_ref.at[p], gout1_ref)
    for _, hand, _ in waits:
        hand()

    upstream = own_g[...].astype(F32)
    hidden = hidden_in[...]
    rows = rows_in[...]
    router_probs = router_in[...]
    lane = lax.broadcasted_iota(jnp.int32, (ROWS, 16), 1)
    chosen = (lane == row_to_column(ids_in[...]) + 2).astype(F32)
    gate = jnp.sum(router_probs * chosen, axis=-1, keepdims=True)
    scale = rms_scale(hidden)
    gain_two = rows[1:2]
    normed = (hidden * scale * gain_two).astype(BF16).astype(F32)
    waits[0][2]()
    result = jnp.sum(col_ref[0].astype(F32), axis=0).astype(BF16).astype(F32)
    d_gate = jnp.sum(upstream * result, axis=-1, keepdims=True)
    d_logits = router_probs * (chosen * d_gate - gate * d_gate)
    d_two = jnp.dot(d_logits, rows, precision=precise, preferred_element_type=F32)
    waits[1][2]()
    d_two += jnp.sum(col_ref[1].astype(F32), axis=0).astype(BF16).astype(F32)
    d_hidden = upstream + norm_back(hidden, scale, gain_two, d_two)
    dh_ref[...] = d_hidden.astype(BF16).reshape(SEQS, SHARD, D)
    wait_dh = share(4, "fsdp", lambda p: dh_ref.at[lax.rem(p, 4)], dhall_ref)
    mixed_ref[...] = (hidden + gate * result).astype(BF16)
    g_gain_two = jnp.sum(d_two * hidden * scale, axis=0, keepdims=True)
    g_router = lax.dot_general(
        d_logits, normed, (((0,), (0,)), ((), ())), precision=precise, preferred_element_type=F32
    )

    wait_gin()
    load_gin = pltpu.make_async_copy(gin1_ref, gin_ref, load.at[8])
    load_gin.start()
    wait_gout()
    load_gout = pltpu.make_async_copy(gout1_ref, gout_ref, load.at[9])
    load_gout.start()
    load_gin.wait()
    gin2_ref[...] = jnp.sum(gin_ref[...].astype(F32), axis=0).astype(BF16)
    wait_gin2 = share(9, "copies", lambda p: gin2_ref.at[p], ginx_ref)
    load_gout.wait()
    gout2_ref[...] = jnp.sum(gout_ref[...].astype(F32), axis=0).astype(BF16)
    wait_gout2 = share(10, "row", lambda p: gout2_ref.at[p], goutx_ref)

    for copy in late:
        copy.wait()
    wait_dh()
    dh = dhall_ref[...].reshape(LEN, D)
    d_att = dot_last(dh, wo_ref[...]).astype(BF16)
    dpre_ref[1, :HW] = dot_rows(att_ref[...].reshape(LEN, HW), dh).astype(BF16)
    gwo_of = lambda p: dpre_ref.at[1, pl.ds(pl.multiple_of(p * 48, 48), 48)]
    wait_gwo = share(5, "row", gwo_of, gwoall_ref)
    for h in range(HG):
        query = qkv_ref[:, h * HD : (h + 1) * HD]
        key = qkv_ref[:, HW + h * HD : HW + (h + 1) * HD]
        value = qkv_ref[:, 2 * HW + h * HD : 2 * HW + (h + 1) * HD]
        d_head = d_att[:, h * HD : (h + 1) * HD]
        probs = probs_ref[h]
        d_probs = dot_last(d_head, value)
        inner = jnp.sum(d_probs * probs, axis=-1, keepdims=True)
        d_scores = (probs * (d_probs - inner)).astype(BF16)
        dqkv_ref[:, h * HD : (h + 1) * HD] = dot(d_scores, key).astype(BF16)
        dqkv_ref[:, HW + h * HD : HW + (h + 1) * HD] = dot_rows(d_scores, query).astype(BF16)
        dqkv_ref[:, 2 * HW + h * HD : 2 * HW + (h + 1) * HD] = dot_rows(
            probs.astype(BF16), d_head
        ).astype(BF16)
        dscores_ref[h] = d_scores
    dqkv = dqkv_ref[...]
    gqkv_ref[...] = dot_rows(norm_ref[...], dqkv).astype(BF16).reshape(FSDP, 48, 3 * HW)
    wait_gqkv = share(6, "fsdp", lambda p: gqkv_ref.at[p], gqkvall_ref)
    part = dot_last(dqkv, w_ref[...].reshape(D, 3 * HW))
    dpre_ref[0, :LEN] = part.astype(BF16)
    part_of = lambda p: dpre_ref.at[0, pl.ds(pl.multiple_of(p * SHARD, SHARD), SHARD)]
    wait_gin2()
    gin2_ref[0] = jnp.sum(ginx_ref[...].astype(F32), axis=0).astype(BF16)
    wait_gin3 = share(13, "copies", lambda p: gin2_ref.at[0], gin3_ref)
    wait_gout2()
    gout2_ref[0] = jnp.sum(goutx_ref[...].astype(F32), axis=0).astype(BF16)
    wait_gout3 = share(14, "copies", lambda p: gout2_ref.at[0], gout3_ref)
    line_ref[...] = jnp.zeros_like(line_ref)
    flip = lax.broadcasted_iota(jnp.int32, (LEN, LEN), 0) + lax.broadcasted_iota(jnp.int32, (LEN, LEN), 1)
    flip = (flip == LEN - 1).astype(BF16)
    for h in range(HG):
        turned = dot(flip, dscores_ref[h])
        wide = jnp.concatenate([turned, jnp.zeros((LEN, LEN), F32)], axis=1)
        wide = pltpu.roll(wide, LEN + 1, 1, stride=1, stride_axis=0)
        line_ref[pl.ds(z * HG + h, 1), :] = jnp.sum(wide, axis=0, keepdims=True)
    x = x_ref[...].astype(F32)
    g_gain_one = jnp.sum(part * x * rms_scale(x), axis=0, keepdims=True)
    index = lax.broadcasted_iota(jnp.int32, (8, D), 0)
    small = jnp.where(index == 0, g_gain_one, jnp.where(index == 1, g_gain_two, 0.0))
    small = jnp.where((index >= 2) & (index < 2 + EXPERTS), g_router[:8], small)
    column = lax.broadcasted_iota(jnp.int32, (FSDP, 8, D), 2)
    first = lax.broadcasted_iota(jnp.int32, (FSDP, 8, D), 0) * 48
    small = jnp.where((column >= first) & (column < first + 48), small[None], 0.0).reshape(FSDP * 8, D)
    smalls = lax.dot_general(
        small, place_ref[...], (((1,), (1,)), ((), ())), precision=precise, preferred_element_type=F32
    ) + lax.dot_general(
        bucket_ref[...], line_ref[...], (((1,), (1,)), ((), ())), precision=precise, preferred_element_type=F32
    )
    smalls_ref[...] = smalls.reshape(FSDP, 8, 128)
    wait_smalls = share(8, "fsdp", lambda p: smalls_ref.at[p], smallsall_ref)

    wait_gwo()
    g_wo = jnp.sum(gwoall_ref[...].astype(F32), axis=0).astype(BF16)
    wait_gqkv()
    for h in range(4):
        total = jnp.sum(gqkvall_ref[4 * h : 4 * h + 4].astype(F32), axis=0).astype(BF16)
        dense_ref[h] = total[:, : 2 * HW]
        dense_ref[4 + h, :, :HW] = total[:, 2 * HW :]
        dense_ref[4 + h, :, HW:] = g_wo[:, h * HW : (h + 1) * HW]
    wait_dense = share(11, "all", lambda p: dense_ref.at[p], denseall_ref)
    wait_part = share(7, "fsdp", part_of, partall_ref)
    wait_smalls()
    mine_ref[...] = jnp.sum(smallsall_ref[...], axis=0)
    wait_mine = share(12, "all", lambda p: mine_ref, mineall_ref)
    wait_part()
    d_one = jnp.concatenate(
        [
            sum(partall_ref[4 * h + s].astype(F32) for h in range(4))
            for s in range(SEQS)
        ],
        axis=0,
    )
    inputs = own_x[...].astype(F32)
    gtokens_ref[...] = d_hidden + norm_back(inputs, rms_scale(inputs), rows[0:1], d_one)
    wait_dense()
    densesum_ref[...] = jnp.sum(denseall_ref[...].astype(F32), axis=0).astype(BF16)
    wait_dense2 = share(15, "all", lambda p: densesum_ref, dense_out)
    wait_mine()
    totals_out[...] = jnp.sum(mineall_ref[...], axis=0)
    wait_gin3()
    wait_gout3()
    wait_dense2()


def back(*arrays):
    vmem, anywhere = pl.BlockSpec(memory_space=pltpu.VMEM), pl.BlockSpec(memory_space=pl.ANY)
    shape, buffer = jax.ShapeDtypeStruct, pltpu.VMEM
    total = 2 * HALF
    return pl.pallas_call(
        back_kernel,
        out_shape=(
            shape((ROWS, D), BF16),
            shape((ROWS, D), F32),
            shape((8, 48, 2 * HW), BF16),
            shape((8, 128), F32),
            shape((4, 2, 48, D), BF16),
            shape((4, 2, 48, D), BF16),
            shape((4, 4, 2, 48, D), BF16),
            shape((4, 4, 2, 48, D), BF16),
        ),
        in_specs=[vmem] * 9 + [anywhere] * 11,
        out_specs=(vmem,) * 6 + (anywhere,) * 2,
        scratch_shapes=[buffer(array.shape, array.dtype) for array in arrays[12:]]
        + [
            buffer((2, total, D), BF16),
            buffer((2, total, D), BF16),
            buffer((total, D), BF16),
            buffer((2, total, D), BF16),
            buffer((2, HALF, D), BF16),
            buffer((2, 4, ROWS, D), BF16),
            buffer((2, 2, ROWS // 2, D), BF16),
            buffer((4, 4, 2, 48, D), BF16),
            buffer((4, 4, 2, 48, D), BF16),
            buffer((4, 2, 48, D), BF16),
            buffer((4, 2, 48, D), BF16),
            buffer((4, 2, 48, D), BF16),
            buffer((4, 2, 48, D), BF16),
            buffer((SEQS, SHARD, D), BF16),
            buffer((FSDP, SHARD, D), BF16),
            buffer((LEN, 3 * HW), BF16),
            buffer((HG, LEN, LEN), BF16),
            buffer((FSDP, SHARD, D), BF16),
            buffer((FSDP, 48, 3 * HW), BF16),
            buffer((FSDP, 48, 3 * HW), BF16),
            buffer((4, 48, D), BF16),
            buffer((128, 2 * LEN), F32),
            buffer((FSDP, 8, 128), F32),
            buffer((FSDP, 8, 128), F32),
            buffer((8, 48, 2 * HW), BF16),
            buffer((8, 48, 2 * HW), BF16),
            buffer((48, 2 * HW), BF16),
            buffer((8, 128), F32),
            buffer((8, 8, 128), F32),
            pltpu.SemaphoreType.DMA((14,)),
            pltpu.SemaphoreType.DMA((2, HALF // CHUNK)),
            pltpu.SemaphoreType.DMA((2, HALF // CHUNK)),
            pltpu.SemaphoreType.DMA((2, 2, 2)),
            pltpu.SemaphoreType.DMA((2, 2, 2)),
            pltpu.SemaphoreType.DMA((16, 16)),
            pltpu.SemaphoreType.DMA((16, 16)),
            pltpu.SemaphoreType.DMA((16,)),
        ],
        compiler_params=pltpu.CompilerParams(
            collective_id=1, has_side_effects=True, vmem_limit_bytes=VMEM_BYTES
        ),
        name="back",
    )(*arrays)


def finish_kernel(
    mixed_ref, tokens_ref, dense_ref, totals_ref, gin_ref, gout_ref,
    mixed_out, tokens_out, gain_one_out, gq_out, gk_out, gv_out, go_out, gbias_out, gain_two_out, router_out,
    gin_out, gout_out,
):
    mixed_out[...] = mixed_ref[...]
    tokens_out[...] = tokens_ref[...]
    totals = totals_ref[...]
    gain_one_out[...] = totals[0:1, :48]
    gain_two_out[...] = totals[1:2, :48]
    router_out[...] = totals[2 : 2 + EXPERTS, :48]
    gbias_out[...] = totals[6:8, :HEADS]
    for h in range(4):
        at = slice(h * HW, (h + 1) * HW)
        first, second = dense_ref[h].astype(F32), dense_ref[4 + h].astype(F32)
        gq_out[:, at], gk_out[:, at] = first[:, :HW], first[:, HW:]
        gv_out[:, at], go_out[:, at] = second[:, :HW], second[:, HW:]
    for q in range(4):
        at = slice(q * 48, (q + 1) * 48)
        gin_out[:, at, :] = gin_ref[q].astype(F32)
        gout_out[:, at, :] = gout_ref[q].astype(F32)


def finish(*arrays):
    vmem, shape = pl.BlockSpec(memory_space=pltpu.VMEM), jax.ShapeDtypeStruct
    return pl.pallas_call(
        finish_kernel,
        out_shape=(
            shape((ROWS, D), BF16),
            shape((ROWS, D), F32),
            shape((1, 48), F32),
            shape((48, D), F32),
            shape((48, D), F32),
            shape((48, D), F32),
            shape((48, D), F32),
            shape((2, HEADS), F32),
            shape((1, 48), F32),
            shape((EXPERTS, 48), F32),
            shape((2, UNITS, D), F32),
            shape((2, UNITS, D), F32),
        ),
        in_specs=[vmem] * 6,
        out_specs=(vmem,) * 12,
        compiler_params=pltpu.CompilerParams(vmem_limit_bytes=VMEM_BYTES),
        name="finish",
    )(*arrays)


def body(
    tokens, lengths, expert_ids, gain_attn, w_query, w_key, w_value, w_output, rel_bias, gain_ffn,
    router, expert_in, expert_out, out_grad,
):
    onehot = bucket_rows()
    tokens, out_grad = tokens[0], out_grad[0].reshape(ROWS, D)
    place = np.zeros((128, D), np.float32)
    place[np.arange(D) % 48, np.arange(D)] = 1.0
    buckets = np.zeros((FSDP, 16, 2 * LEN), np.float32)
    buckets[:, 6:8] = onehot.T.reshape(FSDP, 2, 2 * LEN)
    inputs = tokens.reshape(ROWS, D)
    ids = expert_ids.reshape(1, ROWS)
    (
        x_seq, w_packed, wo_full, normed_one, qkv, attended, probs, hidden_one, router_probs, rows,
        two_all, g_all, facts_all, win_all, wout_all,
    ) = front(
        lengths, ids, jnp.asarray(place), jnp.asarray(buckets.reshape(FSDP * 16, 2 * LEN)),
        inputs, gain_attn.reshape(1, 48), gain_ffn.reshape(1, 48), router.T, rel_bias, w_query, w_key, w_value,
        tokens, w_output, out_grad, expert_in, expert_out,
    )
    backs = np.zeros((FSDP, 8, 2 * LEN), np.float32)
    backs[:, 6:8] = onehot.T.reshape(FSDP, 2, 2 * LEN)
    *parts, _, _ = back(
        facts_all, hidden_one, router_probs, rows, inputs, out_grad, ids,
        jnp.asarray(place), jnp.asarray(backs.reshape(FSDP * 8, 2 * LEN)),
        x_seq.reshape(LEN, D), normed_one, wo_full.reshape(D, D), w_packed, attended, probs, qkv,
        two_all.reshape(8 * ROWS, D), g_all.reshape(8 * ROWS, D), win_all, wout_all,
    )
    mixed, grad_tokens, gain_one, gq, gk, gv, go, bias, gain_two, routing, gin, gout = finish(*parts)
    return (
        mixed.reshape(1, SEQS, SHARD, D),
        grad_tokens.reshape(1, SEQS, SHARD, D),
        gain_one.reshape(48),
        gq,
        gk,
        gv,
        go,
        bias,
        gain_two.reshape(48),
        routing.T,
        gin,
        gout,
    )


def solution(mesh):
    in_specs = (
        P(("replica", "expert"), None, "fsdp", None),
        P(("replica", "expert"), None),
        P(("replica", "expert", "fsdp"), None, None),
        P("fsdp"),
        P("fsdp", None),
        P("fsdp", None),
        P("fsdp", None),
        P("fsdp", None),
        P("fsdp", None),
        P("fsdp"),
        P("fsdp", None),
        P("expert", "fsdp", None),
        P("expert", "fsdp", None),
        P(("replica", "expert"), None, "fsdp", None),
    )
    out_specs = (
        P(("replica", "expert"), None, "fsdp", None),
        P(("replica", "expert"), None, "fsdp", None),
        P("fsdp"),
        P("fsdp", None),
        P("fsdp", None),
        P("fsdp", None),
        P("fsdp", None),
        P("fsdp", None),
        P("fsdp"),
        P("fsdp", None),
        P("expert", "fsdp", None),
        P("expert", "fsdp", None),
    )
    return jax.shard_map(body, mesh=mesh, in_specs=in_specs, out_specs=out_specs, check_vma=False)
```

```python
import functools
import math

import jax
import jax.numpy as jnp
import numpy as np
from jax import lax
from jax.experimental import pallas as pl
from jax.experimental.pallas import tpu as pltpu
from jax.sharding import PartitionSpec as P

MAXDIST = 128
MESH = pl.DeviceIdType.MESH
F32, BF16 = jnp.float32, jnp.bfloat16
precise = lax.Precision.HIGHEST
VMEM_BYTES = 60 * 1024 * 1024

D, HEADS, HD, FF, NB, LEN, SEQS, SHARD, ROWS = 768, 12, 64, 3072, 32, 512, 4, 32, 128
EXPERTS, FSDP, UNITS = 4, 16, 192
HG = 3
HW = HG * HD


def bucket_of(offset):
    per_side, exact = NB // 2, NB // 4
    dist = abs(offset)
    if dist < exact:
        near = dist
    else:
        near = exact + int(math.log(dist / exact) / math.log(MAXDIST / exact) * (per_side - exact))
        near = min(near, per_side - 1)
    return (per_side if offset > 0 else 0) + near


def bucket_rows():
    onehot = np.zeros((2 * LEN, NB), np.float32)
    for index in range(2 * LEN):
        offset = index if index < LEN else index - 2 * LEN
        if offset != -LEN:
            onehot[index, bucket_of(offset)] = 1.0
    return onehot


def fsdp_peer(step, me):
    row = lax.rem(me // 4 + step // 4, 4)
    col = lax.rem(lax.rem(me, 4) + lax.rem(step, 4), 4)
    return row * 4 + col


def dot(left, right):
    return jnp.dot(left, right, preferred_element_type=F32)


def dot_rows(left, right):
    return lax.dot_general(left, right, (((0,), (0,)), ((), ())), preferred_element_type=F32)


def dot_last(left, right):
    return lax.dot_general(left, right, (((1,), (1,)), ((), ())), preferred_element_type=F32)


def gelu_pair(pre):
    cdf = 0.5 * (1.0 + lax.erf(pre * (2.0**-0.5)))
    pdf = jnp.exp(-0.5 * pre * pre) * (1.0 / math.sqrt(2.0 * math.pi))
    return pre * cdf, cdf + pre * pdf


def attention_forward(x_ref, gain, w_ref, bias_ref, bias_row, length, att_ref, probs_ref, qkv_ref, norm_ref):
    x = x_ref[...].reshape(LEN, D).astype(F32)
    scale = lax.rsqrt(jnp.mean(x * x, axis=-1, keepdims=True) + 1e-6)
    normed = (x * scale * gain).astype(BF16)
    norm_ref[...] = normed
    qkv_ref[...] = dot(normed, w_ref[...].reshape(D, 3 * HW)).astype(BF16)
    live = lax.broadcasted_iota(jnp.int32, (LEN, LEN), 1) < length
    for h in range(HG):
        query = qkv_ref[:, h * HD : (h + 1) * HD]
        key = qkv_ref[:, HW + h * HD : HW + (h + 1) * HD]
        value = qkv_ref[:, 2 * HW + h * HD : 2 * HW + (h + 1) * HD]
        line = jnp.broadcast_to(bias_ref[pl.ds(bias_row + h, 1), :], (LEN, 2 * LEN))
        bias = pltpu.roll(line, 0, 1, stride=1, stride_axis=0)[:, :LEN]
        scores = jnp.where(live, dot_last(query, key) + bias, -1e30)
        powers = jnp.exp(scores - jnp.max(scores, axis=-1, keepdims=True))
        probs = powers / jnp.sum(powers, axis=-1, keepdims=True)
        probs_ref[h] = probs
        att = dot(probs.astype(BF16), value).astype(BF16)
        att_ref[:, :, h * HD : (h + 1) * HD] = att.reshape(FSDP, SHARD, HD)


def unpack(small, place):
    wide = dot(small, place).reshape(FSDP, 16, D)
    owner = lax.broadcasted_iota(jnp.int32, (FSDP, 16, D), 2)
    first = lax.broadcasted_iota(jnp.int32, (FSDP, 16, D), 0) * 48
    return jnp.sum(jnp.where((owner >= first) & (owner < first + 48), wide, 0.0), axis=0)


def row_to_column(row):
    return jnp.broadcast_to(row.astype(F32), (ROWS, ROWS)).T[:, :1].astype(jnp.int32)


def front_kernel(
    length_ref, ids_ref, place_ref, bucket_ref, own_x_ref,
    gain_one_ref, gain_two_ref, router_in, bias_in, wq_ref, wk_ref, wv_ref,
    tokens, w_output, out_grad, ein, eout,
    x_out, w_out, wo_out, norm_out, qkv_out, att_out, probs_out, hidden_ref, router_ref, rows_ref,
    two_all, g_all, facts_all, win_all, wout_all,
    x_ref, w_ref, wo_ref, norm_ref, qkv_ref, att_ref, probs_ref, save,
    packed, small, small_ref, back_ref, bias_ref, two_ref, facts_ref,
    send, recv, local, pass_send, pass_recv, cross_send, cross_recv, relay_send, relay_recv,
):
    f, c, r = lax.axis_index("fsdp"), lax.axis_index("expert"), lax.axis_index("replica")
    z, y = f // 4, lax.rem(f, 4)
    other = 1 - c
    sibling = {"expert": other}
    in_col = lambda p: {"fsdp": p * 4 + y}
    in_row = lambda p: {"fsdp": z * 4 + p}
    barrier = pltpu.get_barrier_semaphore()

    def greet(where):
        pl.semaphore_signal(barrier, inc=1, device_id=where, device_id_type=MESH)

    def hello(step, carry):
        greet({"fsdp": fsdp_peer(step, f)})
        return carry

    lax.fori_loop(1, FSDP, hello, 0)
    greet(sibling)
    for step in range(1, 4):
        greet({"fsdp": lax.rem(z + step, 4) * 4 + y, "expert": other})
        greet({"replica": lax.rem(r + step, 4)})
    for h in range(4):
        for side, weight in enumerate((wq_ref, wk_ref, wv_ref)):
            packed[h, :, side * HW : (side + 1) * HW] = weight[:, h * HW : (h + 1) * HW]
    unit = lambda rows: (
        lax.broadcasted_iota(jnp.int32, (rows, 128), 0) == lax.broadcasted_iota(jnp.int32, (rows, 128), 1)
    ).astype(BF16)
    shift = lambda rows, by: (
        lax.broadcasted_iota(jnp.int32, (rows, 16), 0) + by == lax.broadcasted_iota(jnp.int32, (rows, 16), 1)
    ).astype(BF16)
    index = lax.broadcasted_iota(jnp.int32, (16, 128), 0)
    lines = dot_rows(shift(EXPERTS, 2), dot(router_in[...], unit(48)).astype(BF16))
    lines += dot_rows(shift(2, 6), dot(bias_in[...], unit(HEADS)).astype(BF16))
    lines += jnp.where(index == 0, dot(gain_one_ref[...], unit(48)), 0.0)
    lines += jnp.where(index == 1, dot(gain_two_ref[...], unit(48)), 0.0)
    small[...] = lines.astype(BF16)
    pl.semaphore_wait(barrier, FSDP - 1 + 7)

    def remote(k, src, dst, p, slot, where):
        return pltpu.make_async_remote_copy(
            src_ref=src, dst_ref=dst, send_sem=send.at[k, p], recv_sem=recv.at[k, slot],
            device_id=where, device_id_type=MESH,
        )

    def everyone(k, block, out):
        make = lambda p, slot: remote(k, block(p), out.at[slot], p, slot, {"fsdp": p})

        def push(step, carry):
            make(fsdp_peer(step, f), f).start()
            return carry

        def finish(step, carry):
            p = fsdp_peer(step, f)
            copy = make(p, p)
            copy.wait_recv()
            copy.wait_send()
            return carry

        own = pltpu.make_async_copy(block(f), out.at[f], local.at[k])
        lax.fori_loop(1, FSDP, push, 0)
        own.start()

        def wait():
            lax.fori_loop(1, FSDP, finish, 0)
            own.wait()

        return wait

    def ring(k, relay_k, src, out, me, where, cut, passed=lambda block, half: None):
        after, before, across = lax.rem(me + 1, 4), lax.rem(me + 3, 4), lax.rem(me + 2, 4)
        make = lambda p, slot: remote(k, src, out.at[slot], p, slot, where(p))

        def hand(block, half, p):
            there = cut(out.at[block], half)
            return pltpu.make_async_remote_copy(
                src_ref=there, dst_ref=there, send_sem=relay_send.at[relay_k, half],
                recv_sem=relay_recv.at[relay_k, half], device_id=where(p), device_id_type=MESH,
            )

        make(after, me).start()
        make(before, me).start()
        own = pltpu.make_async_copy(src, out.at[me], local.at[k])
        own.start()

        def relay():
            make(before, before).wait_recv()
            hand(before, 0, after).start()
            make(after, after).wait_recv()
            hand(after, 1, before).start()
            for block in (before, after):
                for half in range(2):
                    passed(block, half)

        def wait():
            for half, p in enumerate((after, before)):
                hand(across, half, p).wait_recv()
                passed(across, half)
            make(after, after).wait_send()
            make(before, before).wait_send()
            hand(before, 0, after).wait_send()
            hand(after, 1, before).wait_send()
            own.wait()

        return relay, wait

    def column(k, pass_k, src, out):
        def to_sibling(core, block, half, source=None):
            rows = pl.ds(half * (ROWS // 2), ROWS // 2)
            there = out.at[core * 4 + block, rows]
            return pltpu.make_async_remote_copy(
                src_ref=there if source is None else source.at[rows], dst_ref=there,
                send_sem=pass_send.at[pass_k, block, half], recv_sem=pass_recv.at[pass_k, block, half],
                device_id=sibling, device_id_type=MESH,
            )

        cut = lambda ref, half: ref.at[pl.ds(half * (ROWS // 2), ROWS // 2)]
        passed = lambda block, half: to_sibling(c, block, half).start()
        relay, wait_own = ring(k, pass_k, src, out.at[pl.ds(c * 4, 4)], z, in_col, cut, passed)
        for half in range(2):
            to_sibling(c, z, half, src).start()

        def wait():
            wait_own()
            for block in range(4):
                for half in range(2):
                    to_sibling(c, block, half).wait_send()
                    to_sibling(other, block, half).wait_recv()

        return relay, wait

    wait_x = everyone(0, lambda p: tokens.at[lax.rem(p, 4)], x_ref)
    wait_small = everyone(1, lambda p: small, small_ref)
    wait_w = everyone(2, lambda p: packed.at[p // 4], w_ref)
    quarter = pl.ds(pl.multiple_of(r * 48, 48), 48)
    ring_steps = (1, 3, 2)

    def fetch(p, slot):
        return remote(
            5, eout.at[:, quarter], wout_all.at[slot, :, quarter], p, slot, in_row(p)
        )

    def cross(block, q, part):
        rows = pl.ds(pl.multiple_of(part * 48, 48), 48)
        return pltpu.make_async_remote_copy(
            src_ref=wout_all.at[block, :, rows], dst_ref=wout_all.at[block, :, rows],
            send_sem=cross_send.at[block, q], recv_sem=cross_recv.at[block, part],
            device_id={"replica": q}, device_id_type=MESH,
        )

    for step in ring_steps:
        fetch(lax.rem(y + step, 4), y).start()
    own_wout = pltpu.make_async_copy(eout, wout_all.at[y], local.at[5])
    own_wout.start()

    def cross_all():
        for step in ring_steps:
            block = lax.rem(y + step, 4)
            fetch(block, block).wait_recv()
            for turn in ring_steps:
                cross(block, lax.rem(r + turn, 4), r).start()

    def wait_wout():
        own_wout.wait()
        for step in ring_steps:
            block = lax.rem(y + step, 4)
            fetch(block, block).wait_send()
            for turn in ring_steps:
                q = lax.rem(r + turn, 4)
                cross(block, q, r).wait_send()
                cross(block, q, q).wait_recv()


    wait_small()
    smalls = small_ref[...].reshape(FSDP * 16, 128)
    rows = unpack(smalls, place_ref[...].astype(BF16))
    rows_ref[...] = rows
    bias_ref[...] = dot_rows(smalls, bucket_ref[...].astype(BF16))[:16]
    wait_x()
    wait_w()
    wait_wo = everyone(3, lambda p: w_output, wo_ref)
    forward_g, wait_g = column(6, 0, out_grad, g_all)
    relay_win, wait_win = ring(
        4, 2, ein, win_all, y, in_row, lambda ref, half: ref.at[pl.ds(half, 1)]
    )
    cross_all()
    attention_forward(
        x_ref, rows[0:1], w_ref, bias_ref, HG * z, length_ref[0, y], att_ref, probs_ref, qkv_ref, norm_ref
    )

    wait_att = everyone(7, lambda p: att_ref.at[p], back_ref)
    pairs = (
        (x_ref, x_out), (w_ref, w_out), (norm_ref, norm_out), (qkv_ref, qkv_out), (att_ref, att_out),
        (probs_ref, probs_out), (wo_ref, wo_out),
    )
    saves = [pltpu.make_async_copy(src, dst, save.at[k]) for k, (src, dst) in enumerate(pairs)]
    forward_g()
    for copy in saves[:6]:
        copy.start()
    wait_wo()
    saves[6].start()
    wait_att()
    hidden = own_x_ref[...].astype(F32)
    for h in range(4):
        att = jnp.concatenate([back_ref[h * 4 + s] for s in range(SEQS)], axis=0)
        hidden += dot(att, wo_ref[4 * h : 4 * h + 4].reshape(HW, D))
    hidden_ref[...] = hidden
    scale = lax.rsqrt(jnp.mean(hidden * hidden, axis=-1, keepdims=True) + 1e-6)
    two = (hidden * scale * rows[1:2]).astype(BF16)
    two_ref[...] = two
    forward_two, wait_two = column(8, 1, two_ref, two_all)
    logits = lax.dot_general(
        two.astype(F32), rows, (((1,), (1,)), ((), ())), precision=precise, preferred_element_type=F32
    )
    lane = lax.broadcasted_iota(jnp.int32, (ROWS, 16), 1)
    inside = (lane >= 2) & (lane < 2 + EXPERTS)
    logits = jnp.where(inside, logits, -1e30)
    powers = jnp.where(inside, jnp.exp(logits - jnp.max(logits, axis=-1, keepdims=True)), 0.0)
    router_probs = powers / jnp.sum(powers, axis=-1, keepdims=True)
    router_ref[...] = router_probs
    ids = row_to_column(ids_ref[...])
    gate = jnp.sum(jnp.where(lane == ids + 2, router_probs, 0.0), axis=-1, keepdims=True)
    wide = lax.broadcasted_iota(jnp.int32, (ROWS, ROWS), 1)
    facts = jnp.where(wide == 0, gate, jnp.where(wide == 1, ids.astype(F32), 0.0))
    facts_ref[...] = facts.T[:8]
    me = c * 4 + z
    spots = [(other if i % 2 == 0 else c, lax.rem(z + (i + 1) // 2, 4)) for i in range(7)]
    fact = lambda core, p, slot: remote(
        9, facts_ref, facts_all.at[slot], core * 4 + p, slot, {"fsdp": p * 4 + y, "expert": core}
    )
    for core, p in spots:
        fact(core, p, me).start()
    own_facts = pltpu.make_async_copy(facts_ref, facts_all.at[me], local.at[9])
    own_facts.start()
    forward_two()
    relay_win()
    for copy in saves:
        copy.wait()
    wait_two()
    wait_g()
    wait_win()
    wait_wout()
    for core, p in spots:
        copy = fact(core, p, core * 4 + p)
        copy.wait_recv()
        copy.wait_send()
    own_facts.wait()


def front(lengths, *arrays):
    vmem, smem = pl.BlockSpec(memory_space=pltpu.VMEM), pl.BlockSpec(memory_space=pltpu.SMEM)
    anywhere = pl.BlockSpec(memory_space=pl.ANY)
    shape = jax.ShapeDtypeStruct
    return pl.pallas_call(
        front_kernel,
        out_shape=(
            shape((FSDP, SHARD, D), BF16),
            shape((FSDP, 48, 3 * HW), BF16),
            shape((FSDP, 48, D), BF16),
            shape((LEN, D), BF16),
            shape((LEN, 3 * HW), BF16),
            shape((FSDP, SHARD, HW), BF16),
            shape((HG, LEN, LEN), F32),
            shape((ROWS, D), F32),
            shape((ROWS, 16), F32),
            shape((16, D), F32),
            shape((8, ROWS, D), BF16),
            shape((8, ROWS, D), BF16),
            shape((8, 8, ROWS), F32),
            shape((4, 2, UNITS, D), BF16),
            shape((4, 2, UNITS, D), BF16),
        ),
        in_specs=[smem] + [vmem] * 11 + [anywhere] * 5,
        out_specs=(anywhere,) * 7 + (vmem,) * 3 + (anywhere,) * 5,
        scratch_shapes=[
            pltpu.VMEM((FSDP, SHARD, D), BF16),
            pltpu.VMEM((FSDP, 48, 3 * HW), BF16),
            pltpu.VMEM((FSDP, 48, D), BF16),
            pltpu.VMEM((LEN, D), BF16),
            pltpu.VMEM((LEN, 3 * HW), BF16),
            pltpu.VMEM((FSDP, SHARD, HW), BF16),
            pltpu.VMEM((HG, LEN, LEN), F32),
            pltpu.SemaphoreType.DMA((7,)),
            pltpu.VMEM((4, 48, 3 * HW), BF16),
            pltpu.VMEM((16, 128), BF16),
            pltpu.VMEM((FSDP, 16, 128), BF16),
            pltpu.VMEM((FSDP, SHARD, HW), BF16),
            pltpu.VMEM((16, 2 * LEN), F32),
            pltpu.VMEM((ROWS, D), BF16),
            pltpu.VMEM((8, ROWS), F32),
            pltpu.SemaphoreType.DMA((10, 16)),
            pltpu.SemaphoreType.DMA((10, 16)),
            pltpu.SemaphoreType.DMA((10,)),
            pltpu.SemaphoreType.DMA((2, 4, 2)),
            pltpu.SemaphoreType.DMA((2, 4, 2)),
            pltpu.SemaphoreType.DMA((4, 4)),
            pltpu.SemaphoreType.DMA((4, 4)),
            pltpu.SemaphoreType.DMA((3, 2)),
            pltpu.SemaphoreType.DMA((3, 2)),
        ],
        compiler_params=pltpu.CompilerParams(
            collective_id=0, has_side_effects=True, vmem_limit_bytes=VMEM_BYTES
        ),
        name="front",
    )(lengths, *arrays)


def rms_scale(values):
    return lax.rsqrt(jnp.mean(values * values, axis=-1, keepdims=True) + 1e-6)


def norm_back(values, scale, gain, upstream):
    weighted = upstream * gain
    inner = jnp.mean(values * weighted, axis=-1, keepdims=True)
    return scale * weighted - values * (scale * scale * scale * inner)


HALF = 4 * ROWS
STEP = 256
CHUNK = 64


def back_kernel(
    facts_ref, hidden_in, router_in, rows_in, own_x, own_g, ids_in, place_ref, bucket_ref,
    x_hbm, norm_hbm, wo_hbm, w_hbm, att_hbm, probs_hbm, qkv_hbm, two_hbm, g_hbm, win_hbm, wout_hbm,
    mixed_ref, gtokens_ref, dense_out, totals_out, gin3_ref, gout3_ref, gin1_ref, gout1_ref,
    w_ref, att_ref, probs_ref, qkv_ref, two_ref, g_ref, win_ref, wout_ref,
    acts_ref, dpre_ref, dres_ref, res_ref, pair_ref, col_ref, relay_ref,
    gin_ref, gout_ref, gin2_ref, gout2_ref, ginx_ref, goutx_ref,
    dh_ref, dhall_ref, dqkv_ref, dscores_ref, partall_ref, gqkv_ref, gqkvall_ref, gwoall_ref,
    line_ref, smalls_ref, smallsall_ref, dense_ref, denseall_ref, densesum_ref, mine_ref, mineall_ref,
    load, pair_send, pair_recv, leg_send, leg_recv, send, recv, local,
):
    f, c, r = lax.axis_index("fsdp"), lax.axis_index("expert"), lax.axis_index("replica")
    z, y = f // 4, lax.rem(f, 4)
    other = 1 - c
    me = r * 2 + c
    sibling = {"expert": other}
    in_all = lambda p: {"replica": p // 2, "expert": lax.rem(p, 2)}
    x_ref, norm_ref = acts_ref.at[0, pl.ds(0, LEN)], acts_ref.at[0, pl.ds(LEN, LEN)]
    wo_ref = acts_ref.at[1, pl.ds(0, HW)]
    wo_mine = wo_hbm.at[pl.ds(pl.multiple_of(z * HW, HW), HW)]
    late = [
        pltpu.make_async_copy(src, dst, load.at[k])
        for k, (src, dst) in enumerate(
            zip(
                (w_hbm, att_hbm, probs_hbm, qkv_hbm, x_hbm, norm_hbm, wo_mine),
                (w_ref, att_ref, probs_ref, qkv_ref, x_ref, norm_ref, wo_ref),
            )
        )
    ]
    now = [
        pltpu.make_async_copy(src, dst, load.at[10 + k])
        for k, (src, dst) in enumerate(
            zip((two_hbm, win_hbm, g_hbm, wout_hbm), (two_ref, win_ref, g_ref, wout_ref))
        )
    ]
    for copy in now + late[:4]:
        copy.start()
    barrier = pltpu.get_barrier_semaphore()

    def greet(step, carry):
        where = {"fsdp": fsdp_peer(step, f)}
        pl.semaphore_signal(barrier, inc=1, device_id=where, device_id_type=MESH)
        return carry

    def greet_all(step, carry):
        where = in_all(lax.rem(me + step, 8))
        pl.semaphore_signal(barrier, inc=1, device_id=where, device_id_type=MESH)
        return carry

    lax.fori_loop(1, FSDP, greet, 0)
    lax.fori_loop(1, 8, greet_all, 0)
    pl.semaphore_wait(barrier, FSDP - 1 + 7)

    kinds = {
        "fsdp": (FSDP, f, fsdp_peer, lambda p: {"fsdp": p}),
        "all": (8, me, lambda step, own: lax.rem(own + step, 8), in_all),
        "row": (4, y, lambda step, own: lax.rem(own + step, 4), lambda p: {"fsdp": z * 4 + p}),
        "col": (4, z, lambda step, own: lax.rem(own + step, 4), lambda p: {"fsdp": p * 4 + y}),
        "copies": (4, r, lambda step, own: lax.rem(own + step, 4), lambda p: {"replica": p}),
    }

    def share(k, kind, block, out):
        size, own, peer, where = kinds[kind]

        def make(p, slot):
            return pltpu.make_async_remote_copy(
                src_ref=block(p), dst_ref=out.at[slot], send_sem=send.at[k, p], recv_sem=recv.at[k, slot],
                device_id=where(p), device_id_type=MESH,
            )

        def push(step, carry):
            make(peer(step, own), own).start()
            return carry

        def finish(step, carry):
            p = peer(step, own)
            copy = make(p, p)
            copy.wait_recv()
            copy.wait_send()
            return carry

        lax.fori_loop(1, size, push, 0)
        mine = pltpu.make_async_copy(block(own), out.at[own], local.at[k])
        mine.start()

        def wait():
            lax.fori_loop(1, size, finish, 0)
            mine.wait()

        return wait

    after, before, across = lax.rem(z + 1, 4), lax.rem(z + 3, 4), lax.rem(z + 2, 4)

    def home(side, block):
        half_of = lambda ref, half: ref.at[pl.ds(half * (ROWS // 2), ROWS // 2)]

        def make(p, slot):
            return pltpu.make_async_remote_copy(
                src_ref=block(p), dst_ref=col_ref.at[side, slot], send_sem=send.at[2 + side, p],
                recv_sem=recv.at[2 + side, slot], device_id={"fsdp": p * 4 + y}, device_id_type=MESH,
            )

        def first_leg(half, p):
            return pltpu.make_async_remote_copy(
                src_ref=half_of(block(across), half), dst_ref=relay_ref.at[side, half],
                send_sem=leg_send.at[side, 0, half], recv_sem=leg_recv.at[side, 0, half],
                device_id={"fsdp": p * 4 + y}, device_id_type=MESH,
            )

        def second_leg(half, slot, p):
            return pltpu.make_async_remote_copy(
                src_ref=relay_ref.at[side, half], dst_ref=half_of(col_ref.at[side, slot], half),
                send_sem=leg_send.at[side, 1, half], recv_sem=leg_recv.at[side, 1, half],
                device_id={"fsdp": p * 4 + y}, device_id_type=MESH,
            )

        first_leg(0, after).start()
        first_leg(1, before).start()
        mine = pltpu.make_async_copy(block(z), col_ref.at[side, z], local.at[2 + side])

        def whole():
            make(after, z).start()
            make(before, z).start()
            mine.start()

        def hand():
            first_leg(0, before).wait_recv()
            second_leg(0, before, after).start()
            first_leg(1, after).wait_recv()
            second_leg(1, after, before).start()

        def wait():
            for p in (after, before):
                make(p, p).wait_recv()
                make(p, p).wait_send()
            for half, p in enumerate((after, before)):
                second_leg(half, across, p).wait_recv()
                first_leg(half, p).wait_send()
                second_leg(half, across, p).wait_send()
            mine.wait()

        return whole, hand, wait

    for copy in now:
        copy.wait()
    w_in = [win_ref[:, e].reshape(D, D) for e in range(2)]
    w_out = [wout_ref[:, e].reshape(D, D) for e in range(2)]
    zero = jnp.zeros((), F32)

    def pass_on(core, chunk, side):
        rows = pl.ds(pl.multiple_of(chunk * CHUNK, CHUNK), CHUNK)
        source = pl.ds(pl.multiple_of(core * HALF + chunk * CHUNK, CHUNK), CHUNK)
        return pltpu.make_async_remote_copy(
            src_ref=res_ref.at[side, source], dst_ref=pair_ref.at[side, rows],
            send_sem=pair_send.at[side, chunk], recv_sem=pair_recv.at[side, chunk],
            device_id=sibling, device_id_type=MESH,
        )

    def expert_rows(core, step):
        rows = pl.ds(pl.multiple_of(core * HALF + step * STEP, STEP), STEP)
        x = two_ref[rows, :]
        gates, ids = [], []
        for part in range(STEP // ROWS):
            wide = jnp.concatenate(
                [facts_ref[core * 4 + step * (STEP // ROWS) + part], jnp.zeros((ROWS - 8, ROWS), F32)], axis=0
            ).T
            gates.append(wide[:, 0:1])
            ids.append(wide[:, 1:2])
        gate = jnp.concatenate(gates, axis=0)
        ids = jnp.concatenate(ids, axis=0).astype(jnp.int32) - 2 * c
        d_result = (gate * g_ref[rows, :].astype(F32)).astype(BF16)
        dres_ref[rows, :] = d_result
        is_one = ids == 1
        pre = jnp.where(is_one, dot_last(x, w_in[1]), dot_last(x, w_in[0]))
        acts, slope = gelu_pair(pre)
        d_pre = jnp.where(is_one, dot_last(d_result, w_out[1]), dot_last(d_result, w_out[0])) * slope
        total, back = 0.0, 0.0
        for e in range(2):
            here = ids == e
            acts_e = jnp.where(here, acts, zero).astype(BF16)
            d_pre_e = jnp.where(here, d_pre, zero).astype(BF16)
            acts_ref[e, rows, :] = acts_e
            dpre_ref[e, rows, :] = d_pre_e
            total += dot(acts_e, w_out[e])
            back += dot(d_pre_e, w_in[e])
        res_ref[0, rows, :] = total.astype(BF16)
        res_ref[1, rows, :] = back.astype(BF16)

    def first_rows(step, carry):
        expert_rows(other, step)
        for side in range(2):
            for part in range(STEP // CHUNK):
                pass_on(other, step * (STEP // CHUNK) + part, side).start()
        return carry

    def own_rows(step, carry):
        expert_rows(c, step)
        return carry

    lax.fori_loop(0, HALF // STEP, first_rows, 0)
    lax.fori_loop(0, HALF // STEP, own_rows, 0)
    def arrived(chunk, carry):
        for side in range(2):
            pass_on(other, chunk, side).wait_send()
            pass_on(c, chunk, side).wait_recv()
        return carry

    waits = []
    lax.fori_loop(0, HALF // CHUNK, arrived, 0)
    own_half = pl.ds(pl.multiple_of(c * HALF, HALF), HALF)
    for side in range(2):
        pair_ref[side] += res_ref[side, own_half, :]
        block = lambda p, side=side: pair_ref.at[side, pl.ds(pl.multiple_of(p * ROWS, ROWS), ROWS)]
        waits.append(home(side, block))
    for whole, _, _ in waits:
        whole()
    for e in range(2):
        g_in = dot_rows(dpre_ref[e], two_ref[...]).astype(BF16)
        for p in range(4):
            for q in range(4):
                start = p * UNITS + q * 48
                gin_ref[p, q, e] = g_in[start : start + 48]
    wait_gin = share(0, "row", lambda p: gin_ref.at[p], gin1_ref)
    for e in range(2):
        g_out = dot_rows(acts_ref[e], dres_ref[...]).astype(BF16)
        for p in range(4):
            for q in range(4):
                start = p * UNITS + q * 48
                gout_ref[q, p, e] = g_out[start : start + 48]
    for copy in late[4:]:
        copy.start()
    wait_gout = share(1, "copies", lambda p: gout_ref.at[p], gout1_ref)
    for _, hand, _ in waits:
        hand()

    upstream = own_g[...].astype(F32)
    hidden = hidden_in[...]
    rows = rows_in[...]
    router_probs = router_in[...]
    lane = lax.broadcasted_iota(jnp.int32, (ROWS, 16), 1)
    chosen = (lane == row_to_column(ids_in[...]) + 2).astype(F32)
    gate = jnp.sum(router_probs * chosen, axis=-1, keepdims=True)
    scale = rms_scale(hidden)
    gain_two = rows[1:2]
    normed = (hidden * scale * gain_two).astype(BF16).astype(F32)
    waits[0][2]()
    result = jnp.sum(col_ref[0].astype(F32), axis=0).astype(BF16).astype(F32)
    d_gate = jnp.sum(upstream * result, axis=-1, keepdims=True)
    d_logits = router_probs * (chosen * d_gate - gate * d_gate)
    d_two = jnp.dot(d_logits, rows, precision=precise, preferred_element_type=F32)
    waits[1][2]()
    d_two += jnp.sum(col_ref[1].astype(F32), axis=0).astype(BF16).astype(F32)
    d_hidden = upstream + norm_back(hidden, scale, gain_two, d_two)
    dh_ref[...] = d_hidden.astype(BF16).reshape(SEQS, SHARD, D)
    wait_dh = share(4, "fsdp", lambda p: dh_ref.at[lax.rem(p, 4)], dhall_ref)
    mixed_ref[...] = (hidden + gate * result).astype(BF16)
    g_gain_two = jnp.sum(d_two * hidden * scale, axis=0, keepdims=True)
    g_router = lax.dot_general(
        d_logits, normed, (((0,), (0,)), ((), ())), precision=precise, preferred_element_type=F32
    )

    wait_gin()
    load_gin = pltpu.make_async_copy(gin1_ref, gin_ref, load.at[8])
    load_gin.start()
    wait_gout()
    load_gout = pltpu.make_async_copy(gout1_ref, gout_ref, load.at[9])
    load_gout.start()
    load_gin.wait()
    gin2_ref[...] = jnp.sum(gin_ref[...].astype(F32), axis=0).astype(BF16)
    wait_gin2 = share(9, "copies", lambda p: gin2_ref.at[p], ginx_ref)
    load_gout.wait()
    gout2_ref[...] = jnp.sum(gout_ref[...].astype(F32), axis=0).astype(BF16)
    wait_gout2 = share(10, "row", lambda p: gout2_ref.at[p], goutx_ref)

    for copy in late:
        copy.wait()
    wait_dh()
    dh = dhall_ref[...].reshape(LEN, D)
    d_att = dot_last(dh, wo_ref[...]).astype(BF16)
    dpre_ref[1, :HW] = dot_rows(att_ref[...].reshape(LEN, HW), dh).astype(BF16)
    gwo_of = lambda p: dpre_ref.at[1, pl.ds(pl.multiple_of(p * 48, 48), 48)]
    wait_gwo = share(5, "row", gwo_of, gwoall_ref)
    for h in range(HG):
        query = qkv_ref[:, h * HD : (h + 1) * HD]
        key = qkv_ref[:, HW + h * HD : HW + (h + 1) * HD]
        value = qkv_ref[:, 2 * HW + h * HD : 2 * HW + (h + 1) * HD]
        d_head = d_att[:, h * HD : (h + 1) * HD]
        probs = probs_ref[h]
        d_probs = dot_last(d_head, value)
        inner = jnp.sum(d_probs * probs, axis=-1, keepdims=True)
        d_scores = (probs * (d_probs - inner)).astype(BF16)
        dqkv_ref[:, h * HD : (h + 1) * HD] = dot(d_scores, key).astype(BF16)
        dqkv_ref[:, HW + h * HD : HW + (h + 1) * HD] = dot_rows(d_scores, query).astype(BF16)
        dqkv_ref[:, 2 * HW + h * HD : 2 * HW + (h + 1) * HD] = dot_rows(
            probs.astype(BF16), d_head
        ).astype(BF16)
        dscores_ref[h] = d_scores
    dqkv = dqkv_ref[...]
    gqkv_ref[...] = dot_rows(norm_ref[...], dqkv).astype(BF16).reshape(FSDP, 48, 3 * HW)
    wait_gqkv = share(6, "fsdp", lambda p: gqkv_ref.at[p], gqkvall_ref)
    part = dot_last(dqkv, w_ref[...].reshape(D, 3 * HW))
    dpre_ref[0, :LEN] = part.astype(BF16)
    part_of = lambda p: dpre_ref.at[0, pl.ds(pl.multiple_of(p * SHARD, SHARD), SHARD)]
    wait_part = share(7, "fsdp", part_of, partall_ref)
    wait_gin2()
    gin2_ref[0] = jnp.sum(ginx_ref[...].astype(F32), axis=0).astype(BF16)
    wait_gin3 = share(13, "copies", lambda p: gin2_ref.at[0], gin3_ref)
    wait_gout2()
    gout2_ref[0] = jnp.sum(goutx_ref[...].astype(F32), axis=0).astype(BF16)
    wait_gout3 = share(14, "copies", lambda p: gout2_ref.at[0], gout3_ref)
    line_ref[...] = jnp.zeros_like(line_ref)
    flip = lax.broadcasted_iota(jnp.int32, (LEN, LEN), 0) + lax.broadcasted_iota(jnp.int32, (LEN, LEN), 1)
    flip = (flip == LEN - 1).astype(BF16)
    for h in range(HG):
        turned = dot(flip, dscores_ref[h])
        wide = jnp.concatenate([turned, jnp.zeros((LEN, LEN), F32)], axis=1)
        wide = pltpu.roll(wide, LEN + 1, 1, stride=1, stride_axis=0)
        line_ref[pl.ds(z * HG + h, 1), :] = jnp.sum(wide, axis=0, keepdims=True)
    x = x_ref[...].astype(F32)
    g_gain_one = jnp.sum(part * x * rms_scale(x), axis=0, keepdims=True)
    index = lax.broadcasted_iota(jnp.int32, (8, D), 0)
    small = jnp.where(index == 0, g_gain_one, jnp.where(index == 1, g_gain_two, 0.0))
    small = jnp.where((index >= 2) & (index < 2 + EXPERTS), g_router[:8], small)
    column = lax.broadcasted_iota(jnp.int32, (FSDP, 8, D), 2)
    first = lax.broadcasted_iota(jnp.int32, (FSDP, 8, D), 0) * 48
    small = jnp.where((column >= first) & (column < first + 48), small[None], 0.0).reshape(FSDP * 8, D)
    smalls = lax.dot_general(
        small, place_ref[...], (((1,), (1,)), ((), ())), precision=precise, preferred_element_type=F32
    ) + lax.dot_general(
        bucket_ref[...], line_ref[...], (((1,), (1,)), ((), ())), precision=precise, preferred_element_type=F32
    )
    smalls_ref[...] = smalls.reshape(FSDP, 8, 128)
    wait_smalls = share(8, "fsdp", lambda p: smalls_ref.at[p], smallsall_ref)

    wait_gwo()
    g_wo = jnp.sum(gwoall_ref[...].astype(F32), axis=0).astype(BF16)
    wait_gqkv()
    for h in range(4):
        total = jnp.sum(gqkvall_ref[4 * h : 4 * h + 4].astype(F32), axis=0).astype(BF16)
        dense_ref[h] = total[:, : 2 * HW]
        dense_ref[4 + h, :, :HW] = total[:, 2 * HW :]
        dense_ref[4 + h, :, HW:] = g_wo[:, h * HW : (h + 1) * HW]
    wait_dense = share(11, "all", lambda p: dense_ref.at[p], denseall_ref)
    wait_smalls()
    mine_ref[...] = jnp.sum(smallsall_ref[...], axis=0)
    wait_mine = share(12, "all", lambda p: mine_ref, mineall_ref)
    wait_part()
    d_one = jnp.concatenate(
        [
            sum(partall_ref[4 * h + s].astype(F32) for h in range(4))
            for s in range(SEQS)
        ],
        axis=0,
    )
    inputs = own_x[...].astype(F32)
    gtokens_ref[...] = d_hidden + norm_back(inputs, rms_scale(inputs), rows[0:1], d_one)
    wait_dense()
    densesum_ref[...] = jnp.sum(denseall_ref[...].astype(F32), axis=0).astype(BF16)
    wait_dense2 = share(15, "all", lambda p: densesum_ref, dense_out)
    wait_mine()
    totals_out[...] = jnp.sum(mineall_ref[...], axis=0)
    wait_gin3()
    wait_gout3()
    wait_dense2()


def back(*arrays):
    vmem, anywhere = pl.BlockSpec(memory_space=pltpu.VMEM), pl.BlockSpec(memory_space=pl.ANY)
    shape, buffer = jax.ShapeDtypeStruct, pltpu.VMEM
    total = 2 * HALF
    return pl.pallas_call(
        back_kernel,
        out_shape=(
            shape((ROWS, D), BF16),
            shape((ROWS, D), F32),
            shape((8, 48, 2 * HW), BF16),
            shape((8, 128), F32),
            shape((4, 2, 48, D), BF16),
            shape((4, 2, 48, D), BF16),
            shape((4, 4, 2, 48, D), BF16),
            shape((4, 4, 2, 48, D), BF16),
        ),
        in_specs=[vmem] * 9 + [anywhere] * 11,
        out_specs=(vmem,) * 6 + (anywhere,) * 2,
        scratch_shapes=[buffer(array.shape, array.dtype) for array in arrays[12:]]
        + [
            buffer((2, total, D), BF16),
            buffer((2, total, D), BF16),
            buffer((total, D), BF16),
            buffer((2, total, D), BF16),
            buffer((2, HALF, D), BF16),
            buffer((2, 4, ROWS, D), BF16),
            buffer((2, 2, ROWS // 2, D), BF16),
            buffer((4, 4, 2, 48, D), BF16),
            buffer((4, 4, 2, 48, D), BF16),
            buffer((4, 2, 48, D), BF16),
            buffer((4, 2, 48, D), BF16),
            buffer((4, 2, 48, D), BF16),
            buffer((4, 2, 48, D), BF16),
            buffer((SEQS, SHARD, D), BF16),
            buffer((FSDP, SHARD, D), BF16),
            buffer((LEN, 3 * HW), BF16),
            buffer((HG, LEN, LEN), BF16),
            buffer((FSDP, SHARD, D), BF16),
            buffer((FSDP, 48, 3 * HW), BF16),
            buffer((FSDP, 48, 3 * HW), BF16),
            buffer((4, 48, D), BF16),
            buffer((128, 2 * LEN), F32),
            buffer((FSDP, 8, 128), F32),
            buffer((FSDP, 8, 128), F32),
            buffer((8, 48, 2 * HW), BF16),
            buffer((8, 48, 2 * HW), BF16),
            buffer((48, 2 * HW), BF16),
            buffer((8, 128), F32),
            buffer((8, 8, 128), F32),
            pltpu.SemaphoreType.DMA((14,)),
            pltpu.SemaphoreType.DMA((2, HALF // CHUNK)),
            pltpu.SemaphoreType.DMA((2, HALF // CHUNK)),
            pltpu.SemaphoreType.DMA((2, 2, 2)),
            pltpu.SemaphoreType.DMA((2, 2, 2)),
            pltpu.SemaphoreType.DMA((16, 16)),
            pltpu.SemaphoreType.DMA((16, 16)),
            pltpu.SemaphoreType.DMA((16,)),
        ],
        compiler_params=pltpu.CompilerParams(
            collective_id=1, has_side_effects=True, vmem_limit_bytes=VMEM_BYTES
        ),
        name="back",
    )(*arrays)


def finish_kernel(
    mixed_ref, tokens_ref, dense_ref, totals_ref, gin_ref, gout_ref,
    mixed_out, tokens_out, gain_one_out, gq_out, gk_out, gv_out, go_out, gbias_out, gain_two_out, router_out,
    gin_out, gout_out,
):
    mixed_out[...] = mixed_ref[...]
    tokens_out[...] = tokens_ref[...]
    totals = totals_ref[...]
    gain_one_out[...] = totals[0:1, :48]
    gain_two_out[...] = totals[1:2, :48]
    router_out[...] = totals[2 : 2 + EXPERTS, :48]
    gbias_out[...] = totals[6:8, :HEADS]
    for h in range(4):
        at = slice(h * HW, (h + 1) * HW)
        first, second = dense_ref[h].astype(F32), dense_ref[4 + h].astype(F32)
        gq_out[:, at], gk_out[:, at] = first[:, :HW], first[:, HW:]
        gv_out[:, at], go_out[:, at] = second[:, :HW], second[:, HW:]
    for q in range(4):
        at = slice(q * 48, (q + 1) * 48)
        gin_out[:, at, :] = gin_ref[q].astype(F32)
        gout_out[:, at, :] = gout_ref[q].astype(F32)


def finish(*arrays):
    vmem, shape = pl.BlockSpec(memory_space=pltpu.VMEM), jax.ShapeDtypeStruct
    return pl.pallas_call(
        finish_kernel,
        out_shape=(
            shape((ROWS, D), BF16),
            shape((ROWS, D), F32),
            shape((1, 48), F32),
            shape((48, D), F32),
            shape((48, D), F32),
            shape((48, D), F32),
            shape((48, D), F32),
            shape((2, HEADS), F32),
            shape((1, 48), F32),
            shape((EXPERTS, 48), F32),
            shape((2, UNITS, D), F32),
            shape((2, UNITS, D), F32),
        ),
        in_specs=[vmem] * 6,
        out_specs=(vmem,) * 12,
        compiler_params=pltpu.CompilerParams(vmem_limit_bytes=VMEM_BYTES),
        name="finish",
    )(*arrays)


def body(
    tokens, lengths, expert_ids, gain_attn, w_query, w_key, w_value, w_output, rel_bias, gain_ffn,
    router, expert_in, expert_out, out_grad,
):
    onehot = bucket_rows()
    tokens, out_grad = tokens[0], out_grad[0].reshape(ROWS, D)
    place = np.zeros((128, D), np.float32)
    place[np.arange(D) % 48, np.arange(D)] = 1.0
    buckets = np.zeros((FSDP, 16, 2 * LEN), np.float32)
    buckets[:, 6:8] = onehot.T.reshape(FSDP, 2, 2 * LEN)
    inputs = tokens.reshape(ROWS, D)
    ids = expert_ids.reshape(1, ROWS)
    (
        x_seq, w_packed, wo_full, normed_one, qkv, attended, probs, hidden_one, router_probs, rows,
        two_all, g_all, facts_all, win_all, wout_all,
    ) = front(
        lengths, ids, jnp.asarray(place), jnp.asarray(buckets.reshape(FSDP * 16, 2 * LEN)),
        inputs, gain_attn.reshape(1, 48), gain_ffn.reshape(1, 48), router.T, rel_bias, w_query, w_key, w_value,
        tokens, w_output, out_grad, expert_in, expert_out,
    )
    backs = np.zeros((FSDP, 8, 2 * LEN), np.float32)
    backs[:, 6:8] = onehot.T.reshape(FSDP, 2, 2 * LEN)
    *parts, _, _ = back(
        facts_all, hidden_one, router_probs, rows, inputs, out_grad, ids,
        jnp.asarray(place), jnp.asarray(backs.reshape(FSDP * 8, 2 * LEN)),
        x_seq.reshape(LEN, D), normed_one, wo_full.reshape(D, D), w_packed, attended, probs, qkv,
        two_all.reshape(8 * ROWS, D), g_all.reshape(8 * ROWS, D), win_all, wout_all,
    )
    mixed, grad_tokens, gain_one, gq, gk, gv, go, bias, gain_two, routing, gin, gout = finish(*parts)
    return (
        mixed.reshape(1, SEQS, SHARD, D),
        grad_tokens.reshape(1, SEQS, SHARD, D),
        gain_one.reshape(48),
        gq,
        gk,
        gv,
        go,
        bias,
        gain_two.reshape(48),
        routing.T,
        gin,
        gout,
    )


def solution(mesh):
    in_specs = (
        P(("replica", "expert"), None, "fsdp", None),
        P(("replica", "expert"), None),
        P(("replica", "expert", "fsdp"), None, None),
        P("fsdp"),
        P("fsdp", None),
        P("fsdp", None),
        P("fsdp", None),
        P("fsdp", None),
        P("fsdp", None),
        P("fsdp"),
        P("fsdp", None),
        P("expert", "fsdp", None),
        P("expert", "fsdp", None),
        P(("replica", "expert"), None, "fsdp", None),
    )
    out_specs = (
        P(("replica", "expert"), None, "fsdp", None),
        P(("replica", "expert"), None, "fsdp", None),
        P("fsdp"),
        P("fsdp", None),
        P("fsdp", None),
        P("fsdp", None),
        P("fsdp", None),
        P("fsdp", None),
        P("fsdp"),
        P("fsdp", None),
        P("expert", "fsdp", None),
        P("expert", "fsdp", None),
    )
    return jax.shard_map(body, mesh=mesh, in_specs=in_specs, out_specs=out_specs, check_vma=False)
```
